32 devices in a mesh: energy: 16 (over z, y, x), cell: 2 (over core).
Axes of the slice: x: 2, y: 2, z: 4, core: 2. Of those that a mesh axis runs over, the one named last changes fastest.
Arguments:
- green_pair: float32 [4, 16, 4, 256, 256], P(None, 'energy', 'cell'), may hold values from -4 to 4
- retarded_diag: float32 [2, 16, 4, 256, 256], P(None, 'energy', 'cell'), may hold values from -0.25 to 0.25
- retarded_upper: float32 [2, 16, 4, 256, 256], P(None, 'energy', 'cell'), may hold values from -0.25 to 0.25
- coulomb_diag: float32 [4, 256, 256], P('cell'), may hold values from -0.375 to 0.375
- coulomb_upper: float32 [4, 256, 256], P('cell'), may hold values from -0.375 to 0.375
Outputs:
- lesser_new: float32 [2, 16, 4, 256, 256], P(None, 'energy', 'cell')
The draws below stay inside these ranges and needn't reach their ends.
All inputs are finite; a program needn't handle non-finite values.
Results may differ from the reference program's by a relative error of at most 0.00014.
Values sent between devices are 32-bit elements; how exact they have to be, the bound alone decides.
No kernel may reach another device: no remote copies, remote signals or barrier semaphores. Data moves between devices by JAX's collectives and lax.ppermute only.
A program may use at most 64 MiB of HBM per device.

```python
import math
import jax
import jax.numpy as jnp
from jax import lax

B = 256
NE = 16
NC = 4


def level_of(own_key, shape, cuts, least, largest):
    gain = 1.0
    for axis_at, shards_of in cuts:
        draws = jax.random.uniform(jax.random.fold_in(jax.random.fold_in(own_key, 6), axis_at), (shards_of,), jnp.float32, least / len(cuts), largest / len(cuts))
        gain = gain * jnp.repeat(jnp.exp(draws), shape[axis_at] // shards_of).reshape((-1,) + (1,) * (len(shape) - 1 - axis_at))
    return gain


def bell_draw(own_key, dims, width, reach, split=(), held_as=jnp.bfloat16):
    gain = level_of(own_key, dims, split, -0.22, 0.18) if split else 1.0
    values = jax.random.normal(own_key, dims, jnp.float32) * width * gain
    return jnp.minimum(jnp.maximum(values, -reach), reach).astype(held_as)


def setup_inputs(seed: int = 0) -> dict:
    arg_keys = jax.random.split(jax.random.key(seed), 6)
    return {
        "green_pair": bell_draw(arg_keys[0], (4, NE, NC, B, B), 0.5, 4.0, ((1, 16), (2, 2)), jnp.float32),
        "retarded_diag": bell_draw(arg_keys[1], (2, NE, NC, B, B), (2 * B) ** -0.5, 0.25, ((1, 16), (2, 2)), jnp.float32),
        "retarded_upper": bell_draw(arg_keys[2], (2, NE, NC, B, B), (2 * B) ** -0.5, 0.25, ((1, 16), (2, 2)), jnp.float32),
        "coulomb_diag": bell_draw(arg_keys[3], (NC, B, B), B ** -0.5, 0.375, ((0, 2),), jnp.float32),
        "coulomb_upper": bell_draw(arg_keys[4], (NC, B, B), B ** -0.5, 0.375, ((0, 2),), jnp.float32),
    }


highest = lax.Precision.HIGHEST

def shift_prev(values, dimension):
    widths = [(0, 0)] * values.ndim
    widths[dimension] = (1, 0)
    length = values.shape[dimension]
    return lax.slice_in_dim(jnp.pad(values, widths), 0, length, axis=dimension)

def shift_next(values, dimension):
    widths = [(0, 0)] * values.ndim
    widths[dimension] = (0, 1)
    length = values.shape[dimension]
    return lax.slice_in_dim(jnp.pad(values, widths), 1, length + 1, axis=dimension)

def outer_real(left, middle):
    inner = jnp.einsum('cab,ecbd->ecad', left, middle, precision=highest)
    return jnp.einsum('ecad,cfd->ecaf', inner, left, precision=highest)

def outer_complex(left_real, left_imaginary, mid_real, mid_imaginary):
    first_real = jnp.einsum('ecab,ecbd->ecad', left_real, mid_real, precision=highest) - jnp.einsum('ecab,ecbd->ecad', left_imaginary, mid_imaginary, precision=highest)
    first_imaginary = jnp.einsum('ecab,ecbd->ecad', left_real, mid_imaginary, precision=highest) + jnp.einsum('ecab,ecbd->ecad', left_imaginary, mid_real, precision=highest)
    out_real = jnp.einsum('ecad,ecfd->ecaf', first_real, left_real, precision=highest) + jnp.einsum('ecad,ecfd->ecaf', first_imaginary, left_imaginary, precision=highest)
    out_imaginary = jnp.einsum('ecad,ecfd->ecaf', first_imaginary, left_real, precision=highest) - jnp.einsum('ecad,ecfd->ecaf', first_real, left_imaginary, precision=highest)
    return (out_real, out_imaginary)

def reference(green_pair, retarded_diag, retarded_upper, coulomb_diag, coulomb_upper):
    scaling = 1.0 / math.sqrt(NE)
    lesser = green_pair[0] + 1j * green_pair[1]
    greater = green_pair[2] + 1j * green_pair[3]
    lesser_hat = jnp.fft.fft(lesser, axis=0)
    greater_hat = jnp.fft.fft(greater, axis=0)
    correlated = jnp.fft.ifft(lesser_hat * jnp.conj(greater_hat), axis=0)
    pol_real = -jnp.imag(correlated) * scaling
    pol_imaginary = jnp.real(correlated) * scaling
    coulomb_symmetric = (coulomb_diag + jnp.swapaxes(coulomb_diag, 1, 2)) * 0.5
    coulomb_lower = jnp.swapaxes(shift_prev(coulomb_upper, 0), 1, 2)
    screened = []
    for plane in (pol_real, pol_imaginary):
        total = outer_real(coulomb_symmetric, plane)
        total = total + outer_real(coulomb_upper, shift_next(plane, 1))
        total = total + outer_real(coulomb_lower, shift_prev(plane, 1))
        screened.append(total)
    screened_hat = jnp.fft.fft(screened[0] + 1j * screened[1], axis=0)
    convolved = jnp.fft.ifft(lesser_hat * screened_hat, axis=0)
    sigma_real = -jnp.imag(convolved) * scaling
    sigma_imaginary = jnp.real(convolved) * scaling
    retarded_lower = jnp.swapaxes(shift_prev(retarded_upper, 2), 3, 4)
    out_real, out_imaginary = outer_complex(retarded_diag[0], retarded_diag[1], sigma_real, sigma_imaginary)
    next_real, next_imaginary = outer_complex(retarded_upper[0], retarded_upper[1], shift_next(sigma_real, 1), shift_next(sigma_imaginary, 1))
    prev_real, prev_imaginary = outer_complex(retarded_lower[0], retarded_lower[1], shift_prev(sigma_real, 1), shift_prev(sigma_imaginary, 1))
    out_real = out_real + next_real + prev_real
    out_imaginary = out_imaginary + next_imaginary + prev_imaginary
    return jnp.stack([out_real, out_imaginary]).astype(jnp.float32)
```

```python
import functools
import math

import jax
import jax.numpy as jnp
from jax import lax
from jax.experimental import pallas as pl
from jax.experimental.pallas import tpu as pltpu
from jax.sharding import PartitionSpec as P

VMEM = pl.BlockSpec(memory_space=pltpu.VMEM)
f32 = jnp.float32
bf16 = jnp.bfloat16


def times_root(value, turn, points, sign):
    re, im = value
    turn = turn % points
    if turn == 0:
        return value
    if 4 * turn == points:
        return (-im, re) if sign > 0 else (im, -re)
    if 2 * turn == points:
        return (-re, -im)
    if 4 * turn == 3 * points:
        return (im, -re) if sign > 0 else (-im, re)
    angle = 2.0 * math.pi * turn / points
    c, s = math.cos(angle), sign * math.sin(angle)
    if 8 * turn % points == 0:
        unit = abs(c)
        a = re if c > 0 else -re
        b = im if c > 0 else -im
        if (s > 0) == (c > 0):
            return ((a - b) * unit, (a + b) * unit)
        return ((a + b) * unit, (b - a) * unit)
    return (re * c - im * s, re * s + im * c)


def fourier(values, sign):
    points = len(values)
    if points == 1:
        return values
    if points % 2:
        out = []
        for k in range(points):
            total = values[0]
            for n in range(1, points):
                term = times_root(values[n], k * n, points, sign)
                total = (total[0] + term[0], total[1] + term[1])
            out.append(total)
        return out
    even = fourier(values[0::2], sign)
    odd = fourier(values[1::2], sign)
    low, high = [], []
    for k in range(points // 2):
        a = even[k]
        b = times_root(odd[k], k, points, sign)
        low.append((a[0] + b[0], a[1] + b[1]))
        high.append((a[0] - b[0], a[1] - b[1]))
    return low + high


def tiles_of(cells, rows, lanes):
    step_rows = 8 if rows % 8 == 0 else rows
    step_lanes = 128 if lanes % 128 == 0 else lanes
    return [
        (c, pl.ds(r, step_rows), pl.ds(b, step_lanes))
        for c in range(cells)
        for r in range(0, rows, step_rows)
        for b in range(0, lanes, step_lanes)
    ]


def polarize_kernel(scaling, entries, lesser_hat, polar_hat):
    points, _, cells, rows, lanes = entries.shape
    for c, r, b in tiles_of(cells, rows, lanes):
        hats = []
        for pair in (0, 2):
            hats.append(
                fourier([(entries[n, pair, c, r, b], entries[n, pair + 1, c, r, b]) for n in range(points)], -1)
            )
            if pair == 0:
                for k in range(points):
                    lesser_hat[k, 0, c, r, b] = hats[0][k][0]
                    lesser_hat[k, 1, c, r, b] = hats[0][k][1]
        for k in range(points):
            greater_re, greater_im = hats[1][k]
            lesser_re = lesser_hat[k, 0, c, r, b]
            lesser_im = lesser_hat[k, 1, c, r, b]
            polar_hat[k, 0, c, r, b] = (lesser_re * greater_im - lesser_im * greater_re) * scaling
            polar_hat[k, 1, c, r, b] = (lesser_re * greater_re + lesser_im * greater_im) * scaling


def convolve_kernel(factor, lesser_hat, screened_hat, sigma):
    points, _, cells, rows, lanes = screened_hat.shape
    for c, r, b in tiles_of(cells, rows, lanes):
        spectral = []
        for k in range(points):
            lesser_re, lesser_im = lesser_hat[k, 0, c, r, b], lesser_hat[k, 1, c, r, b]
            w_re, w_im = screened_hat[k, 0, c, r, b], screened_hat[k, 1, c, r, b]
            spectral.append(
                ((lesser_re * w_re - lesser_im * w_im) * factor, (lesser_re * w_im + lesser_im * w_re) * factor)
            )
        for n, (re, im) in enumerate(fourier(spectral, 1)):
            sigma[n, 0, c, r, b] = -im
            sigma[n, 1, c, r, b] = re


def parts(matrix):
    high = matrix.astype(bf16)
    return (high, (matrix - high.astype(f32)).astype(bf16))


def join(pieces, axis):
    return tuple(jnp.concatenate(p, axis) for p in zip(*pieces, strict=True))


def negative(pair):
    return tuple(-p for p in pair)


def product(left, right, turned=False):
    dims = (((1,), (1 if turned else 0,)), ((), ()))
    dot = functools.partial(lax.dot_general, dimension_numbers=dims, preferred_element_type=f32)
    return dot(left[0], right[0]) + (dot(left[0], right[1]) + dot(left[1], right[0]))


def block_of(ref, plane, cell):
    slabs, _, _, rows, lanes = ref.shape
    return ref[:, plane, cell].reshape(slabs * rows, lanes)


def neighbours(cells, here, before, after):
    previous = [(before, 0)] + [(here, c) for c in range(cells - 1)]
    following = [(here, c) for c in range(1, cells)] + [(after, 0)]
    return previous, following


def screen_kernel(here, before, after, diag, upper, lower, out):
    slabs, planes, cells, rows, lanes = here.shape
    previous, following = neighbours(cells, here, before, after)
    for c in range(cells):
        symmetric = (diag[c] + diag[c].T) * 0.5
        lefts, inners = [], []
        for matrix, (ref, cell) in (
            (symmetric, (here, c)),
            (upper[c], following[c]),
            (lower[c].T, previous[c]),
        ):
            left = parts(matrix)
            lefts.append(left)
            stacked = jnp.concatenate([block_of(ref, p, cell) for p in range(planes)], 0)
            inners.append(parts(product(parts(stacked), left, True)))
        left = join(lefts, 1)
        for p in range(planes):
            inner = join([tuple(q[p * lanes : (p + 1) * lanes] for q in i) for i in inners], 0)
            out[:, p, c] = product(left, inner).reshape(slabs, rows, lanes)


def output_kernel(here, before, after, diag, upper, lower, out):
    _, planes, cells, _, lanes = here.shape
    previous, following = neighbours(cells, here, before, after)
    for c in range(cells):
        total = None
        for matrix, turned, (ref, cell) in (
            (diag, False, (here, c)),
            (upper, False, following[c]),
            (lower, True, previous[c]),
        ):
            re, im = matrix[0, 0, c], matrix[1, 0, c]
            if turned:
                re, im = re.T, im.T
            re, im = parts(re), parts(im)
            middle = parts(jnp.concatenate([block_of(ref, p, cell) for p in range(planes)], 0))
            left = join([join([re, negative(im)], 1), join([im, re], 1)], 0)
            inner = parts(product(left, middle))
            inner_re = tuple(q[:lanes] for q in inner)
            inner_im = tuple(q[lanes:] for q in inner)
            rows = join([join([inner_re, inner_im], 1), join([inner_im, negative(inner_re)], 1)], 0)
            term = product(rows, join([re, im], 1), True)
            total = term if total is None else total + term
        out[0, 0, c] = total[:lanes]
        out[1, 0, c] = total[lanes:]


def call(kernel, outs, *args):
    return pl.pallas_call(
        kernel,
        out_shape=outs,
        in_specs=[VMEM] * len(args),
        out_specs=jax.tree.map(lambda _: VMEM, outs),
        compiler_params=pltpu.CompilerParams(vmem_limit_bytes=48 * 1024 * 1024),
    )(*args)


def shape(dims):
    return jax.ShapeDtypeStruct(tuple(dims), f32)


def exchange(values):
    return lax.all_to_all(values, "energy", split_axis=0, concat_axis=0, tiled=True)


def shifted(block, axis, step):
    count = lax.axis_size(axis)
    route = [(i, i + step) for i in range(count) if 0 <= i + step < count]
    return lax.ppermute(block, axis, route)


def halo(values):
    return (shifted(values[:, :, -1:], "cell", 1), shifted(values[:, :, :1], "cell", -1))


def per_device(green_pair, retarded_diag, retarded_upper, coulomb_diag, coulomb_upper):
    devices = lax.axis_size("energy")
    _, held, cells, orbitals, _ = green_pair.shape
    points = devices * held
    scaling = 1.0 / math.sqrt(points)
    rows = orbitals // devices
    coulomb_edge = shifted(coulomb_upper[-1:], "cell", 1)
    retarded_edge = shifted(retarded_upper[:, :, -1:], "cell", 1)
    coulomb_before = jnp.concatenate([coulomb_edge, coulomb_upper[:-1]], 0)
    retarded_before = jnp.concatenate([retarded_edge, retarded_upper[:, :, :-1]], 2)
    slabs = green_pair.reshape(4, cells, devices, rows, orbitals).transpose(2, 0, 1, 3, 4)
    entries = exchange(slabs)
    half = shape((points, 2, cells, rows, orbitals))
    lesser_hat, polar_hat = call(functools.partial(polarize_kernel, scaling), (half, half), entries)
    polar = exchange(polar_hat)
    screened = call(screen_kernel, half, polar, *halo(polar), coulomb_diag, coulomb_upper, coulomb_before)
    screened_hat = exchange(screened)
    sigma_entries = call(functools.partial(convolve_kernel, scaling / points), half, lesser_hat, screened_hat)
    sigma = exchange(sigma_entries)
    return call(
        output_kernel,
        shape(retarded_diag.shape),
        sigma,
        *halo(sigma),
        retarded_diag,
        retarded_upper,
        retarded_before,
    )


def solution(mesh):
    over_both = P(None, "energy", "cell", None, None)
    over_cell = P("cell", None, None)
    return jax.shard_map(
        per_device,
        mesh=mesh,
        in_specs=(over_both, over_both, over_both, over_cell, over_cell),
        out_specs=over_both,
        check_vma=False,
    )
```

```python
import functools
import math

import jax
import jax.numpy as jnp
from jax import lax
from jax.experimental import pallas as pl
from jax.experimental.pallas import tpu as pltpu
from jax.sharding import PartitionSpec as P

VMEM = pl.BlockSpec(memory_space=pltpu.VMEM)
f32 = jnp.float32
bf16 = jnp.bfloat16


def times_root(value, turn, points, sign):
    re, im = value
    turn = turn % points
    if turn == 0:
        return value
    if 4 * turn == points:
        return (-im, re) if sign > 0 else (im, -re)
    if 2 * turn == points:
        return (-re, -im)
    if 4 * turn == 3 * points:
        return (im, -re) if sign > 0 else (-im, re)
    angle = 2.0 * math.pi * turn / points
    c, s = math.cos(angle), sign * math.sin(angle)
    if 8 * turn % points == 0:
        unit = abs(c)
        a = re if c > 0 else -re
        b = im if c > 0 else -im
        if (s > 0) == (c > 0):
            return ((a - b) * unit, (a + b) * unit)
        return ((a + b) * unit, (b - a) * unit)
    return (re * c - im * s, re * s + im * c)


def fourier(values, sign):
    points = len(values)
    if points == 1:
        return values
    if points % 2:
        out = []
        for k in range(points):
            total = values[0]
            for n in range(1, points):
                term = times_root(values[n], k * n, points, sign)
                total = (total[0] + term[0], total[1] + term[1])
            out.append(total)
        return out
    even = fourier(values[0::2], sign)
    odd = fourier(values[1::2], sign)
    low, high = [], []
    for k in range(points // 2):
        a = even[k]
        b = times_root(odd[k], k, points, sign)
        low.append((a[0] + b[0], a[1] + b[1]))
        high.append((a[0] - b[0], a[1] - b[1]))
    return low + high


def tiles_of(cells, rows, lanes):
    step_rows = 8 if rows % 8 == 0 else rows
    step_lanes = 128 if lanes % 128 == 0 else lanes
    return [
        (c, pl.ds(r, step_rows), pl.ds(b, step_lanes))
        for c in range(cells)
        for r in range(0, rows, step_rows)
        for b in range(0, lanes, step_lanes)
    ]


def polarize_kernel(scaling, entries, lesser_hat, polar_hat):
    points, _, cells, rows, lanes = entries.shape
    for c, r, b in tiles_of(cells, rows, lanes):
        hats = []
        for pair in (0, 2):
            hats.append(
                fourier([(entries[n, pair, c, r, b], entries[n, pair + 1, c, r, b]) for n in range(points)], -1)
            )
            if pair == 0:
                for k in range(points):
                    lesser_hat[k, 0, c, r, b] = hats[0][k][0]
                    lesser_hat[k, 1, c, r, b] = hats[0][k][1]
        for k in range(points):
            greater_re, greater_im = hats[1][k]
            lesser_re = lesser_hat[k, 0, c, r, b]
            lesser_im = lesser_hat[k, 1, c, r, b]
            polar_hat[k, 0, c, r, b] = (lesser_re * greater_im - lesser_im * greater_re) * scaling
            polar_hat[k, 1, c, r, b] = (lesser_re * greater_re + lesser_im * greater_im) * scaling


def convolve_kernel(factor, lesser_hat, screened_hat, sigma):
    points, _, cells, rows, lanes = screened_hat.shape
    for c, r, b in tiles_of(cells, rows, lanes):
        spectral = []
        for k in range(points):
            lesser_re, lesser_im = lesser_hat[k, 0, c, r, b], lesser_hat[k, 1, c, r, b]
            w_re, w_im = screened_hat[k, 0, c, r, b], screened_hat[k, 1, c, r, b]
            spectral.append(
                ((lesser_re * w_re - lesser_im * w_im) * factor, (lesser_re * w_im + lesser_im * w_re) * factor)
            )
        for n, (re, im) in enumerate(fourier(spectral, 1)):
            sigma[n, 0, c, r, b] = -im
            sigma[n, 1, c, r, b] = re


def parts(matrix):
    high = matrix.astype(bf16)
    return (high, (matrix - high.astype(f32)).astype(bf16))


def join(pieces, axis):
    return tuple(jnp.concatenate(p, axis) for p in zip(*pieces, strict=True))


def negative(pair):
    return tuple(-p for p in pair)


def product(left, right, turned=False):
    dims = (((1,), (1 if turned else 0,)), ((), ()))
    dot = functools.partial(lax.dot_general, dimension_numbers=dims, preferred_element_type=f32)
    return dot(left[0], right[0]) + (dot(left[0], right[1]) + dot(left[1], right[0]))


def block_of(ref, plane, cell):
    slabs, _, _, rows, lanes = ref.shape
    return ref[:, plane, cell].reshape(slabs * rows, lanes)


def terms_of(cells, here, received, diag, upper, edges):
    terms = []
    for c in range(cells):
        terms.append((c, functools.partial(diag, c), functools.partial(block_of, here, cell=c)))
        if c + 1 < cells:
            terms.append((c, functools.partial(upper, c), functools.partial(block_of, here, cell=c + 1)))
            terms.append((c + 1, functools.partial(upper, c, turned=True), functools.partial(block_of, here, cell=c)))
    for target, matrix, ref in zip(*edges, received, strict=True):
        terms.append((target, matrix, functools.partial(block_of, ref, cell=0)))
    return terms


def screen_kernel(halos, targets, *refs):
    here, diag, upper = refs[:3]
    received, matrices, out = refs[3 : 3 + halos], refs[3 + halos : -1], refs[-1]
    slabs, planes, cells, rows, lanes = here.shape

    def symmetric(c):
        return (diag[c] + diag[c].T) * 0.5

    def above(c, turned=False):
        return upper[c].T if turned else upper[c]

    edges = ([targets[i] for i in range(halos)], [lambda m=m: m[...] for m in matrices])
    by_cell, others = {}, []
    for target, matrix, read in terms_of(cells, here, received, symmetric, above, edges):
        left = parts(matrix())
        stacked = parts(jnp.concatenate([read(plane=p) for p in range(planes)], 0))
        term = (left, parts(product(stacked, left, True)))
        if isinstance(target, int):
            by_cell.setdefault(target, []).append(term)
        else:
            others.append((target, [term]))
    for target, terms in list(by_cell.items()) + others:
        left = join([t[0] for t in terms], 1)
        for p in range(planes):
            inner = join([tuple(q[p * lanes : (p + 1) * lanes] for q in t[1]) for t in terms], 0)
            total = product(left, inner).reshape(slabs, rows, lanes)
            if isinstance(target, int):
                out[:, p, target] = total
            else:
                out[:, p, target] = out[:, p, target] + total


def output_kernel(halos, targets, *refs):
    here, diag, upper = refs[:3]
    received, matrices, out = refs[3 : 3 + halos], refs[3 + halos : -1], refs[-1]
    _, planes, cells, _, lanes = here.shape

    def pair(ref, c, turned=False):
        re, im = ref[0, 0, c], ref[1, 0, c]
        return (re.T, im.T) if turned else (re, im)

    edges = ([targets[i] for i in range(halos)], [lambda m=m: (m[0], m[1]) for m in matrices])
    totals = {}
    for target, matrix, read in terms_of(
        cells, here, received, functools.partial(pair, diag), functools.partial(pair, upper), edges
    ):
        re, im = (parts(m) for m in matrix())
        middle = parts(jnp.concatenate([read(plane=p) for p in range(planes)], 0))
        left = join([join([re, negative(im)], 1), join([im, re], 1)], 0)
        inner = parts(product(left, middle))
        inner_re = tuple(q[:lanes] for q in inner)
        inner_im = tuple(q[lanes:] for q in inner)
        rows = join([join([inner_re, inner_im], 1), join([inner_im, negative(inner_re)], 1)], 0)
        term = product(rows, join([re, im], 1), True)
        if isinstance(target, int):
            totals[target] = totals[target] + term if target in totals else term
        else:
            for c, total in totals.items():
                out[0, 0, c] = total[:lanes]
                out[1, 0, c] = total[lanes:]
            totals = {}
            out[0, 0, target] = out[0, 0, target] + term[:lanes]
            out[1, 0, target] = out[1, 0, target] + term[lanes:]
    for c, total in totals.items():
        out[0, 0, c] = total[:lanes]
        out[1, 0, c] = total[lanes:]


def call(kernel, outs, *args, scalars=False):
    first = [pl.BlockSpec(memory_space=pltpu.SMEM)] if scalars else []
    return pl.pallas_call(
        kernel,
        out_shape=outs,
        in_specs=first + [VMEM] * (len(args) - len(first)),
        out_specs=jax.tree.map(lambda _: VMEM, outs),
        compiler_params=pltpu.CompilerParams(vmem_limit_bytes=24 * 1024 * 1024),
    )(*args)


def shape(dims):
    return jax.ShapeDtypeStruct(tuple(dims), f32)


def exchange(values):
    return lax.all_to_all(values, "energy", split_axis=0, concat_axis=0, tiled=True)


def shifted(block, axis, step):
    count = lax.axis_size(axis)
    route = [(i, i + step) for i in range(count) if 0 <= i + step < count]
    return lax.ppermute(block, axis, route)


def swapped(block):
    return lax.ppermute(block, "cell", [(0, 1), (1, 0)])


def halo(values):
    count = lax.axis_size("cell")
    if count == 1:
        return []
    head, tail = values[:, :, :1], values[:, :, -1:]
    if count == 2:
        return [swapped(jnp.where(lax.axis_index("cell") == 0, tail, head))]
    return [shifted(tail, "cell", 1), shifted(head, "cell", -1)]


def halo_targets(cells):
    count = lax.axis_size("cell")
    if count == 2:
        targets = [jnp.where(lax.axis_index("cell") == 0, cells - 1, 0)]
    else:
        targets = [0, cells - 1]
    return jnp.stack([jnp.asarray(t, jnp.int32) for t in targets])


def halo_matrices(last_upper):
    count = lax.axis_size("cell")
    if count == 1:
        return []
    before = jnp.swapaxes(shifted(last_upper, "cell", 1), -1, -2)
    if count == 2:
        return [jnp.where(lax.axis_index("cell") == 0, last_upper, before)]
    return [before, last_upper]


def per_device(green_pair, retarded_diag, retarded_upper, coulomb_diag, coulomb_upper):
    devices = lax.axis_size("energy")
    _, held, cells, orbitals, _ = green_pair.shape
    points = devices * held
    scaling = 1.0 / math.sqrt(points)
    rows = orbitals // devices
    targets = halo_targets(cells)
    coulomb_edges = halo_matrices(coulomb_upper[-1])
    retarded_edges = halo_matrices(retarded_upper[:, 0, -1])
    halos = len(coulomb_edges)
    slabs = green_pair.reshape(4, cells, devices, rows, orbitals).transpose(2, 0, 1, 3, 4)
    entries = exchange(slabs)
    half = shape((points, 2, cells, rows, orbitals))
    lesser_hat, polar_hat = call(functools.partial(polarize_kernel, scaling), (half, half), entries)
    polar = exchange(polar_hat)
    screened = call(
        functools.partial(screen_kernel, halos),
        half,
        targets,
        polar,
        coulomb_diag,
        coulomb_upper,
        *halo(polar),
        *coulomb_edges,
        scalars=True,
    )
    screened_hat = exchange(screened)
    sigma_entries = call(functools.partial(convolve_kernel, scaling / points), half, lesser_hat, screened_hat)
    sigma = exchange(sigma_entries)
    return call(
        functools.partial(output_kernel, halos),
        shape(retarded_diag.shape),
        targets,
        sigma,
        retarded_diag,
        retarded_upper,
        *halo(sigma),
        *retarded_edges,
        scalars=True,
    )


def solution(mesh):
    over_both = P(None, "energy", "cell", None, None)
    over_cell = P("cell", None, None)
    return jax.shard_map(
        per_device,
        mesh=mesh,
        in_specs=(over_both, over_both, over_both, over_cell, over_cell),
        out_specs=over_both,
        check_vma=False,
    )
```

```python
import functools
import math

import jax
import jax.numpy as jnp
from jax import lax
from jax.experimental import pallas as pl
from jax.experimental.pallas import tpu as pltpu
from jax.sharding import PartitionSpec as P

VMEM = pl.BlockSpec(memory_space=pltpu.VMEM)
f32 = jnp.float32
bf16 = jnp.bfloat16


def times_root(value, turn, points, sign):
    re, im = value
    turn = turn % points
    if turn == 0:
        return value
    if 4 * turn == points:
        return (-im, re) if sign > 0 else (im, -re)
    if 2 * turn == points:
        return (-re, -im)
    if 4 * turn == 3 * points:
        return (im, -re) if sign > 0 else (-im, re)
    angle = 2.0 * math.pi * turn / points
    c, s = math.cos(angle), sign * math.sin(angle)
    if 8 * turn % points == 0:
        unit = abs(c)
        a = re if c > 0 else -re
        b = im if c > 0 else -im
        if (s > 0) == (c > 0):
            return ((a - b) * unit, (a + b) * unit)
        return ((a + b) * unit, (b - a) * unit)
    return (re * c - im * s, re * s + im * c)


def fourier(values, sign):
    points = len(values)
    if points == 1:
        return values
    if points % 2:
        out = []
        for k in range(points):
            total = values[0]
            for n in range(1, points):
                term = times_root(values[n], k * n, points, sign)
                total = (total[0] + term[0], total[1] + term[1])
            out.append(total)
        return out
    even = fourier(values[0::2], sign)
    odd = fourier(values[1::2], sign)
    low, high = [], []
    for k in range(points // 2):
        a = even[k]
        b = times_root(odd[k], k, points, sign)
        low.append((a[0] + b[0], a[1] + b[1]))
        high.append((a[0] - b[0], a[1] - b[1]))
    return low + high


def tiles_of(rows, lanes):
    step_rows = 8 if rows % 8 == 0 else rows
    step_lanes = 128 if lanes % 128 == 0 else lanes
    return [
        (pl.ds(r, step_rows), pl.ds(b, step_lanes))
        for r in range(0, rows, step_rows)
        for b in range(0, lanes, step_lanes)
    ]


def spectrum(read, points, sign):
    return fourier([read(n) for n in range(points)], sign)


def split_of(devices):
    inner = next(i for i in range(math.isqrt(devices), 0, -1) if devices % i == 0)
    return inner, devices // inner


def along_outer(blocks, inner):
    devices = lax.axis_size("energy")
    return [
        lax.ppermute(b, "energy", [(e, (e + s * inner) % devices) for e in range(devices)]) if s else b
        for s, b in enumerate(blocks)
    ]


def along_inner(blocks, inner):
    devices = lax.axis_size("energy")
    return [
        lax.ppermute(b, "energy", [(e, e - e % inner + (e + t) % inner) for e in range(devices)]) if t else b
        for t, b in enumerate(blocks)
    ]


def pack_kernel(outer, inner, place, *refs):
    blocks, outs = refs[:outer], refs[outer:]
    for t in range(inner):
        to = lax.rem(place[1] + t, inner)
        for s in range(outer):
            outs[t][lax.rem(place[0] + outer - s, outer)] = blocks[s][:, to]


def exchange(place, blocks, inner):
    outer = len(blocks)
    arrived = along_outer(blocks, inner)
    q, _, rows, lanes = blocks[0].shape
    packed = call(
        functools.partial(pack_kernel, outer, inner), [shape((outer, q, rows, lanes))] * inner, place, *arrived
    )
    return along_inner(packed, inner)


def gather(place, arrived, write):
    inner = len(arrived)
    for t, ref in enumerate(arrived):
        origin = lax.rem(place[1] + inner - t, inner)
        for z in range(ref.shape[0]):
            write(z * inner + origin, ref[z])


def emit(place, outs, inner, read):
    outer = len(outs)
    for s, out in enumerate(outs):
        out[...] = read(pl.multiple_of(lax.rem(place[0] + s, outer) * inner, inner), inner)


def polarize_kernel(scaling, inner, groups, place, *refs):
    arrived, lesser_hat, entries, polar = refs[:inner], refs[inner], refs[-2], refs[-1]
    outs = refs[inner + 1 : -2]
    outer = len(outs) // len(groups)
    points, _, rows, lanes = entries.shape

    def write(n, block):
        entries[n] = block

    gather(place, arrived, write)
    for r, b in tiles_of(rows, lanes):
        lesser = spectrum(lambda n: (entries[n, 0, r, b], entries[n, 1, r, b]), points, -1)
        for k, (re, im) in enumerate(lesser):
            lesser_hat[k, 0, r, b] = re
            lesser_hat[k, 1, r, b] = im
        greater = spectrum(lambda n: (entries[n, 2, r, b], entries[n, 3, r, b]), points, -1)
        for k, (re, im) in enumerate(greater):
            lesser_re, lesser_im = lesser_hat[k, 0, r, b], lesser_hat[k, 1, r, b]
            polar[0, k, r, b] = (lesser_re * im - lesser_im * re) * scaling
            polar[1, k, r, b] = (lesser_re * re + lesser_im * im) * scaling
    for g, planes in enumerate(groups):
        emit(
            place,
            outs[g * outer : (g + 1) * outer],
            inner,
            lambda start, count, planes=planes: polar[pl.ds(planes[0], len(planes)), pl.ds(start, count)],
        )


def convolve_kernel(factor, inner, cell, place, *refs):
    screened = (refs[:inner], refs[inner : 2 * inner])
    lesser_hat, outs, entries, sigma = refs[2 * inner], refs[2 * inner + 1 : -2], refs[-2], refs[-1]
    points, _, rows, lanes = entries.shape

    def write_re(k, block):
        entries[k, 0] = block[cell]

    def write_im(k, block):
        entries[k, 1] = block[0]

    gather(place, screened[0], write_re)
    gather(place, screened[1], write_im)
    for r, b in tiles_of(rows, lanes):

        def spectral(k):
            lesser_re, lesser_im = lesser_hat[k, 0, r, b], lesser_hat[k, 1, r, b]
            w_re, w_im = entries[k, 0, r, b], entries[k, 1, r, b]
            return ((lesser_re * w_re - lesser_im * w_im) * factor, (lesser_re * w_im + lesser_im * w_re) * factor)

        for n, (re, im) in enumerate(spectrum(spectral, points, 1)):
            sigma[0, n, r, b] = -im
            sigma[1, n, r, b] = re
    emit(place, outs, inner, lambda start, count: sigma[:, pl.ds(start, count)])


def parts(matrix):
    high = matrix.astype(bf16)
    return (high, (matrix - high.astype(f32)).astype(bf16))


def join(pieces, axis):
    return tuple(jnp.concatenate(p, axis) for p in zip(*pieces, strict=True))


def negative(pair):
    return tuple(-p for p in pair)


def product(left, right, turned=False):
    dims = (((1,), (1 if turned else 0,)), ((), ()))
    dot = functools.partial(lax.dot_general, dimension_numbers=dims, preferred_element_type=f32)
    return dot(left[0], right[0]) + (dot(left[0], right[1]) + dot(left[1], right[0]))


def gather_kernel(inner, cells, plane, halos, place, *refs):
    here, edges = refs[inner * cells], refs[inner * cells + 1 :]
    for c in range(cells):

        def write(e, block, c=c):
            here[c, e] = block[plane[c]]

        gather(place, refs[c * inner : (c + 1) * inner], write)
    for i in range(halos):
        edges[i][...] = here[place[2 + halos + i]]


def screen_kernel(inner, groups, halos, place, *refs):
    here, diag, upper = refs[:3]
    received, matrices = refs[3 : 3 + halos], refs[3 + halos : 3 + 2 * halos]
    outs, total = refs[3 + 2 * halos : -1], refs[-1]
    outer = len(outs) // len(groups)
    cells, devices, rows, lanes = here.shape

    def block(ref, *at):
        return ref[at].reshape(devices * rows, lanes) if at else ref[...].reshape(devices * rows, lanes)

    def inner_of(left, middle):
        return parts(product(parts(middle), left, True))

    for c in range(cells):
        terms = [((diag[c] + diag[c].T) * 0.5, block(here, c))]
        if c + 1 < cells:
            terms.append((upper[c], block(here, c + 1)))
        if c:
            terms.append((upper[c - 1].T, block(here, c - 1)))
        lefts = [parts(m) for m, _ in terms]
        inners = [inner_of(left, x) for left, (_, x) in zip(lefts, terms, strict=True)]
        total[c] = product(join(lefts, 1), join(inners, 0)).reshape(devices, rows, lanes)
    for i in range(halos):
        left = parts(matrices[i][...])
        term = product(left, inner_of(left, block(received[i]))).reshape(devices, rows, lanes)
        total[place[2 + i]] = total[place[2 + i]] + term
    for g, members in enumerate(groups):
        emit(
            place,
            outs[g * outer : (g + 1) * outer],
            inner,
            lambda start, count, members=members: total[pl.ds(members[0], len(members)), pl.ds(start, count)],
        )


def complex_outer(matrix, middle):
    re, im = (parts(m) for m in matrix)
    lanes = middle.shape[1]
    left = join([join([re, negative(im)], 1), join([im, re], 1)], 0)
    inner = parts(product(left, parts(middle)))
    inner_re = tuple(q[:lanes] for q in inner)
    inner_im = tuple(q[lanes:] for q in inner)
    rows = join([join([inner_re, inner_im], 1), join([inner_im, negative(inner_re)], 1)], 0)
    return product(rows, join([re, im], 1), True)


def edges_kernel(inner, cells, halos, place, *refs):
    for i, edge in enumerate(refs[inner * cells :]):
        for c in range(cells):

            @pl.when(place[2 + halos + i] == c)
            def _(edge=edge, c=c):
                def write(e, block):
                    edge[:, e] = block

                gather(place, refs[c * inner : (c + 1) * inner], write)


def output_kernel(inner, cell, place, *refs):
    arrived, diag, upper = refs[:inner], refs[inner], refs[inner + 1]
    before, out, sigma = refs[inner + 2 : -2], refs[-2], refs[-1]
    cells = out.shape[2]
    _, devices, rows, lanes = sigma.shape

    def write(e, block):
        sigma[:, e] = block

    gather(place, arrived, write)
    middle = sigma[...].reshape(2 * devices * rows, lanes)
    terms = [(cell, (diag[0, 0, cell], diag[1, 0, cell]))]
    if cell:
        terms.append((cell - 1, (upper[0, 0, cell - 1], upper[1, 0, cell - 1])))
    if cell + 1 < cells:
        terms.append((cell + 1, (upper[0, 0, cell].T, upper[1, 0, cell].T)))
    added = {target: complex_outer(matrix, middle) for target, matrix in terms}
    for c in range(cells):
        for p in range(2):
            value = added[c][p * lanes : (p + 1) * lanes] if c in added else None
            if before:
                value = before[0][p, 0, c] if value is None else before[0][p, 0, c] + value
            out[p, 0, c] = jnp.zeros((lanes, lanes), f32) if value is None else value


def finish_kernel(halos, place, *refs):
    before, received, matrices, out = refs[0], refs[1 : 1 + halos], refs[1 + halos : -1], refs[-1]
    out[...] = before[...]
    for i in range(halos):
        planes, devices, rows, lanes = received[i].shape
        middle = received[i][...].reshape(planes * devices * rows, lanes)
        term = complex_outer((matrices[i][0], matrices[i][1]), middle)
        c = place[2 + i]
        for p in range(2):
            out[p, 0, c] = out[p, 0, c] + term[p * lanes : (p + 1) * lanes]


def call(kernel, outs, place, *args, scratch=(), **more):
    return pl.pallas_call(
        kernel,
        out_shape=outs,
        in_specs=[pl.BlockSpec(memory_space=pltpu.SMEM)] + [VMEM] * len(args),
        out_specs=jax.tree.map(lambda _: VMEM, outs),
        scratch_shapes=[pltpu.VMEM(dims, f32) for dims in scratch],
        compiler_params=pltpu.CompilerParams(vmem_limit_bytes=24 * 1024 * 1024),
        **more,
    )(place, *args)


def shape(dims):
    return jax.ShapeDtypeStruct(tuple(dims), f32)


def shifted(block, step):
    count = lax.axis_size("cell")
    return lax.ppermute(block, "cell", [(i, i + step) for i in range(count) if 0 <= i + step < count])


def halo_cells(cells):
    count = lax.axis_size("cell")
    if count == 1:
        return []
    if count == 2:
        edge = jnp.where(lax.axis_index("cell") == 0, cells - 1, 0)
        return [edge, edge]
    return [0, cells - 1, cells - 1, 0]


def from_neighbours(edges):
    if lax.axis_size("cell") == 2:
        return [lax.ppermute(edges[0], "cell", [(0, 1), (1, 0)])]
    return [shifted(edge, step) for edge, step in zip(edges, (1, -1), strict=False)]


def halo_matrices(last_upper):
    count = lax.axis_size("cell")
    if count == 1:
        return []
    before = jnp.swapaxes(shifted(last_upper, 1), -1, -2)
    if count == 2:
        return [jnp.where(lax.axis_index("cell") == 0, last_upper, before)]
    return [before, last_upper]


def per_device(green_pair, retarded_diag, retarded_upper, coulomb_diag, coulomb_upper):
    devices = lax.axis_size("energy")
    outer, inner = split_of(devices)
    _, held, cells, orbitals, _ = green_pair.shape
    points = devices * held
    scaling = 1.0 / math.sqrt(points)
    rows = orbitals // devices
    me = lax.axis_index("energy")
    z, r = me // inner, me % inner
    borders = halo_cells(cells)
    halos = len(borders) // 2
    place = jnp.stack([jnp.asarray(v, jnp.int32) for v in [z, r, *borders]])
    coulomb_edges = halo_matrices(coulomb_upper[-1])
    retarded_edges = halo_matrices(retarded_upper[:, 0, -1])

    def block(q):
        return shape((q, inner, rows, orbitals))

    lesser_hat, polar = [], []
    arrived = []
    for c in range(cells):
        green = green_pair[:, 0, c].reshape(4, devices, rows, orbitals)
        blocks = [
            lax.dynamic_slice_in_dim(green, (z + s) % outer * inner, inner, axis=1) for s in range(outer)
        ]
        arrived.append(exchange(place, blocks, inner))
    for c in range(cells):
        groups = ((0, 1),) if c + 1 < cells else ((0,), (1,))
        hat, *blocks = call(
            functools.partial(polarize_kernel, scaling, inner, groups),
            [shape((points, 2, rows, orbitals))] + [block(len(g)) for g in groups for _ in range(outer)],
            place,
            *arrived[c],
            scratch=((points, 4, rows, orbitals), (2, points, rows, orbitals)),
        )
        lesser_hat.append(hat)
        got = [exchange(place, blocks[i : i + outer], inner) for i in range(0, len(blocks), outer)]
        polar.append([(got[0], 0), (got[0], 1)] if len(groups) == 1 else [(got[0], 0), (got[1], 0)])
    screened = []
    for plane in range(2):
        sources = [polar[c][plane] for c in range(cells)]
        here, *edges = call(
            functools.partial(gather_kernel, inner, cells, [q for _, q in sources], halos),
            [shape((cells, devices, rows, orbitals))] + [shape((devices, rows, orbitals))] * halos,
            place,
            *[b for blocks, _ in sources for b in blocks],
        )
        groups = (tuple(range(cells)),) if plane == 0 else tuple((c,) for c in range(cells))
        blocks = call(
            functools.partial(screen_kernel, inner, groups, halos),
            [block(len(g)) for g in groups for _ in range(outer)],
            place,
            here,
            coulomb_diag,
            coulomb_upper,
            *from_neighbours(edges),
            *coulomb_edges,
            scratch=((cells, devices, rows, orbitals),),
        )
        screened.append([exchange(place, blocks[i : i + outer], inner) for i in range(0, len(blocks), outer)])
    sigma = []
    for c in range(cells):
        blocks = call(
            functools.partial(convolve_kernel, scaling / points, inner, c),
            [block(2)] * outer,
            place,
            *screened[0][0],
            *screened[1][c],
            lesser_hat[c],
            scratch=((points, 2, rows, orbitals), (2, points, rows, orbitals)),
        )
        sigma.append(exchange(place, blocks, inner))
    edges = call(
        functools.partial(edges_kernel, inner, cells, halos),
        [shape((2, devices, rows, orbitals))] * halos,
        place,
        *[b for blocks in sigma for b in blocks],
    )
    received = from_neighbours(edges)
    total = []
    for c in range(cells):
        total = [
            call(
                functools.partial(output_kernel, inner, c),
                shape(retarded_diag.shape),
                place,
                *sigma[c],
                retarded_diag,
                retarded_upper,
                *total,
                scratch=((2, devices, rows, orbitals),),
            )
        ]
    return call(functools.partial(finish_kernel, halos), shape(retarded_diag.shape), place, *total, *received, *retarded_edges)


def solution(mesh):
    over_both = P(None, "energy", "cell", None, None)
    over_cell = P("cell", None, None)
    return jax.shard_map(
        per_device,
        mesh=mesh,
        in_specs=(over_both, over_both, over_both, over_cell, over_cell),
        out_specs=over_both,
        check_vma=False,
    )
```

```python
import functools
import math

import jax
import jax.numpy as jnp
from jax import lax
from jax.experimental import pallas as pl
from jax.experimental.pallas import tpu as pltpu
from jax.sharding import PartitionSpec as P

VMEM = pl.BlockSpec(memory_space=pltpu.VMEM)
f32 = jnp.float32
bf16 = jnp.bfloat16


def times_root(value, turn, points, sign):
    re, im = value
    turn = turn % points
    if turn == 0:
        return value
    if 4 * turn == points:
        return (-im, re) if sign > 0 else (im, -re)
    if 2 * turn == points:
        return (-re, -im)
    if 4 * turn == 3 * points:
        return (im, -re) if sign > 0 else (-im, re)
    angle = 2.0 * math.pi * turn / points
    c, s = math.cos(angle), sign * math.sin(angle)
    if 8 * turn % points == 0:
        unit = abs(c)
        a = re if c > 0 else -re
        b = im if c > 0 else -im
        if (s > 0) == (c > 0):
            return ((a - b) * unit, (a + b) * unit)
        return ((a + b) * unit, (b - a) * unit)
    return (re * c - im * s, re * s + im * c)


def fourier(values, sign):
    points = len(values)
    if points == 1:
        return values
    if points % 2:
        out = []
        for k in range(points):
            total = values[0]
            for n in range(1, points):
                term = times_root(values[n], k * n, points, sign)
                total = (total[0] + term[0], total[1] + term[1])
            out.append(total)
        return out
    even = fourier(values[0::2], sign)
    odd = fourier(values[1::2], sign)
    low, high = [], []
    for k in range(points // 2):
        a = even[k]
        b = times_root(odd[k], k, points, sign)
        low.append((a[0] + b[0], a[1] + b[1]))
        high.append((a[0] - b[0], a[1] - b[1]))
    return low + high


def tiles_of(cells, rows, lanes):
    step_rows = 8 if rows % 8 == 0 else rows
    step_lanes = 128 if lanes % 128 == 0 else lanes
    return [
        (c, pl.ds(r, step_rows), pl.ds(b, step_lanes))
        for c in range(cells)
        for r in range(0, rows, step_rows)
        for b in range(0, lanes, step_lanes)
    ]


def polarize_kernel(scaling, entries, lesser_hat, polar_hat):
    points, _, cells, rows, lanes = entries.shape
    for c, r, b in tiles_of(cells, rows, lanes):
        hats = []
        for pair in (0, 2):
            hats.append(
                fourier([(entries[n, pair, c, r, b], entries[n, pair + 1, c, r, b]) for n in range(points)], -1)
            )
            if pair == 0:
                for k in range(points):
                    lesser_hat[k, 0, c, r, b] = hats[0][k][0]
                    lesser_hat[k, 1, c, r, b] = hats[0][k][1]
        for k in range(points):
            greater_re, greater_im = hats[1][k]
            lesser_re = lesser_hat[k, 0, c, r, b]
            lesser_im = lesser_hat[k, 1, c, r, b]
            polar_hat[k, 0, c, r, b] = (lesser_re * greater_im - lesser_im * greater_re) * scaling
            polar_hat[k, 1, c, r, b] = (lesser_re * greater_re + lesser_im * greater_im) * scaling


def convolve_kernel(factor, lesser_hat, screened_hat, sigma):
    points, _, cells, rows, lanes = screened_hat.shape
    for c, r, b in tiles_of(cells, rows, lanes):
        spectral = []
        for k in range(points):
            lesser_re, lesser_im = lesser_hat[k, 0, c, r, b], lesser_hat[k, 1, c, r, b]
            w_re, w_im = screened_hat[k, 0, c, r, b], screened_hat[k, 1, c, r, b]
            spectral.append(
                ((lesser_re * w_re - lesser_im * w_im) * factor, (lesser_re * w_im + lesser_im * w_re) * factor)
            )
        for n, (re, im) in enumerate(fourier(spectral, 1)):
            sigma[n, 0, c, r, b] = -im
            sigma[n, 1, c, r, b] = re


def parts(matrix):
    high = matrix.astype(bf16)
    return (high, (matrix - high.astype(f32)).astype(bf16))


def join(pieces, axis):
    return tuple(jnp.concatenate(p, axis) for p in zip(*pieces, strict=True))


def negative(pair):
    return tuple(-p for p in pair)


def product(left, right, turned=False):
    dims = (((1,), (1 if turned else 0,)), ((), ()))
    dot = functools.partial(lax.dot_general, dimension_numbers=dims, preferred_element_type=f32)
    return dot(left[0], right[0]) + (dot(left[0], right[1]) + dot(left[1], right[0]))


def block_of(ref, plane, cell):
    slabs, _, _, rows, lanes = ref.shape
    return ref[:, plane, cell].reshape(slabs * rows, lanes)


def local_terms(cells):
    terms = [(c, c, c) for c in range(cells)]
    for c in range(cells - 1):
        terms.append((c, c + 1, cells + 2 * c))
        terms.append((c + 1, c, cells + 2 * c + 1))
    return sorted(terms)


def matrices_kernel(cells, halos, place, *refs):
    c_diag, c_upper, r_diag, r_upper, c_edge, r_edge = refs[:6]
    c_high, c_low, r_high, r_low = refs[6:]

    def store(ref, i, matrix):
        for out, part in zip(ref, parts(matrix), strict=True):
            out[i] = part

    def fill(refs, read_diag, read_upper, edge):
        for c in range(cells):
            store(refs, c, read_diag(c))
        for c in range(cells - 1):
            store(refs, cells + 2 * c, read_upper(c))
            store(refs, cells + 2 * c + 1, read_upper(c).T)
        first = 3 * cells - 2
        if halos == 1:
            store(refs, first, jnp.where(place[1] == 0, read_upper(cells - 1), edge.T))
        if halos == 2:
            store(refs, first, edge.T)
            store(refs, first + 1, read_upper(cells - 1))

    fill((c_high, c_low), lambda c: (c_diag[c] + c_diag[c].T) * 0.5, lambda c: c_upper[c], c_edge[...])
    for p in range(2):
        fill(
            (r_high.at[p], r_low.at[p]),
            lambda c, p=p: r_diag[p, 0, c],
            lambda c, p=p: r_upper[p, 0, c],
            r_edge[p],
        )


def real_terms(high, low, terms, read, planes):
    lefts, inners = [], []
    for source, i in terms:
        left = (high[i], low[i])
        stacked = parts(jnp.concatenate([read(p, source) for p in range(planes)], 0))
        lefts.append(left)
        inners.append(parts(product(stacked, left, True)))
    left = join(lefts, 1)
    lanes = high.shape[-1]
    return [
        product(left, join([tuple(q[p * lanes : (p + 1) * lanes] for q in i) for i in inners], 0))
        for p in range(planes)
    ]


def complex_terms(high, low, terms, read):
    total = None
    for source, i in terms:
        re, im = (high[0, i], low[0, i]), (high[1, i], low[1, i])
        lanes = re[0].shape[0]
        middle = parts(jnp.concatenate([read(p, source) for p in range(2)], 0))
        left = join([join([re, negative(im)], 1), join([im, re], 1)], 0)
        inner = parts(product(left, middle))
        inner_re = tuple(q[:lanes] for q in inner)
        inner_im = tuple(q[lanes:] for q in inner)
        rows = join([join([inner_re, inner_im], 1), join([inner_im, negative(inner_re)], 1)], 0)
        term = product(rows, join([re, im], 1), True)
        total = term if total is None else total + term
    return total


def screen_kernel(here, high, low, out):
    slabs, planes, cells, rows, lanes = here.shape
    for c in range(cells):
        terms = [(source, i) for target, source, i in local_terms(cells) if target == c]
        sums = real_terms(high, low, terms, lambda p, source: block_of(here, p, source), planes)
        for p, total in enumerate(sums):
            out[:, p, c] = total.reshape(slabs, rows, lanes)


def screen_halo_kernel(halos, place, before, *refs):
    received, high, low, out = refs[:halos], refs[halos], refs[halos + 1], refs[halos + 2]
    slabs, planes, cells, rows, lanes = out.shape
    for h in range(halos):
        terms = [(0, 3 * cells - 2 + h)]
        sums = real_terms(high, low, terms, lambda p, source, h=h: block_of(received[h], p, source), planes)
        c = place[2 + h]
        for p, total in enumerate(sums):
            out[:, p, c] = before[:, p, c] + total.reshape(slabs, rows, lanes)


def output_kernel(here, high, low, out):
    cells, lanes = here.shape[2], here.shape[4]
    for c in range(cells):
        terms = [(source, i) for target, source, i in local_terms(cells) if target == c]
        total = complex_terms(high, low, terms, lambda p, source: block_of(here, p, source))
        for p in range(2):
            out[p, 0, c] = total[p * lanes : (p + 1) * lanes]


def output_halo_kernel(halos, place, before, *refs):
    received, high, low, out = refs[:halos], refs[halos], refs[halos + 1], refs[halos + 2]
    cells, lanes = out.shape[2], out.shape[4]
    out[...] = before[...]
    for h in range(halos):
        terms = [(0, 3 * cells - 2 + h)]
        total = complex_terms(high, low, terms, lambda p, source, h=h: block_of(received[h], p, source))
        c = place[2 + h]
        for p in range(2):
            out[p, 0, c] = out[p, 0, c] + total[p * lanes : (p + 1) * lanes]


def call(kernel, outs, *args, scalars=False, **more):
    first = [pl.BlockSpec(memory_space=pltpu.SMEM)] if scalars else []
    return pl.pallas_call(
        kernel,
        out_shape=outs,
        in_specs=first + [VMEM] * (len(args) - len(first)),
        out_specs=jax.tree.map(lambda _: VMEM, outs),
        compiler_params=pltpu.CompilerParams(vmem_limit_bytes=24 * 1024 * 1024),
        **more,
    )(*args)


def shape(dims):
    return jax.ShapeDtypeStruct(tuple(dims), f32)


def exchange(values):
    return lax.all_to_all(values, "energy", split_axis=0, concat_axis=0, tiled=True)


def shifted(block, axis, step):
    count = lax.axis_size(axis)
    route = [(i, i + step) for i in range(count) if 0 <= i + step < count]
    return lax.ppermute(block, axis, route)


def swapped(block):
    return lax.ppermute(block, "cell", [(0, 1), (1, 0)])


def halo(values):
    count = lax.axis_size("cell")
    if count == 1:
        return []
    head, tail = values[:, :, :1], values[:, :, -1:]
    if count == 2:
        return [swapped(jnp.where(lax.axis_index("cell") == 0, tail, head))]
    return [shifted(tail, "cell", 1), shifted(head, "cell", -1)]


def place_of(cells):
    count, index = lax.axis_size("cell"), lax.axis_index("cell")
    if count == 1:
        targets = []
    elif count == 2:
        targets = [jnp.where(index == 0, cells - 1, 0)]
    else:
        targets = [0, cells - 1]
    return len(targets), jnp.stack([jnp.asarray(v, jnp.int32) for v in [len(targets), index, *targets]])


def per_device(green_pair, retarded_diag, retarded_upper, coulomb_diag, coulomb_upper):
    devices = lax.axis_size("energy")
    _, held, cells, orbitals, _ = green_pair.shape
    points = devices * held
    scaling = 1.0 / math.sqrt(points)
    rows = orbitals // devices
    halos, place = place_of(cells)
    count = 3 * cells - 2 + halos
    part = jax.ShapeDtypeStruct((count, orbitals, orbitals), bf16)
    pair = jax.ShapeDtypeStruct((2, count, orbitals, orbitals), bf16)
    matrices = call(
        functools.partial(matrices_kernel, cells, halos),
        (part, part, pair, pair),
        place,
        coulomb_diag,
        coulomb_upper,
        retarded_diag,
        retarded_upper,
        shifted(coulomb_upper[-1], "cell", 1),
        shifted(retarded_upper[:, 0, -1], "cell", 1),
        scalars=True,
        cost_estimate=pl.CostEstimate(flops=10**9, bytes_accessed=16 * count * orbitals**2 * 4, transcendentals=0),
    )
    slabs = green_pair.reshape(4, cells, devices, rows, orbitals).transpose(2, 0, 1, 3, 4)
    entries, matrices = lax.optimization_barrier((exchange(slabs), matrices))
    coulomb, retarded = matrices[:2], matrices[2:]
    half = shape((points, 2, cells, rows, orbitals))
    lesser_hat, polar_hat = call(functools.partial(polarize_kernel, scaling), (half, half), entries)
    polar = exchange(polar_hat)
    received = halo(polar)
    screened = call(screen_kernel, half, polar, *coulomb)
    if halos:
        screened = call(
            functools.partial(screen_halo_kernel, halos),
            half,
            place,
            screened,
            *received,
            *coulomb,
            scalars=True,
            input_output_aliases={1: 0},
        )
    screened_hat = exchange(screened)
    sigma = exchange(call(functools.partial(convolve_kernel, scaling / points), half, lesser_hat, screened_hat))
    received = halo(sigma)
    out = call(output_kernel, shape(retarded_diag.shape), sigma, *retarded)
    if halos:
        out = call(
            functools.partial(output_halo_kernel, halos), shape(out.shape), place, out, *received, *retarded, scalars=True
        )
    return out


def solution(mesh):
    over_both = P(None, "energy", "cell", None, None)
    over_cell = P("cell", None, None)
    return jax.shard_map(
        per_device,
        mesh=mesh,
        in_specs=(over_both, over_both, over_both, over_cell, over_cell),
        out_specs=over_both,
        check_vma=False,
    )
```

```python
import functools
import math

import jax
import jax.numpy as jnp
from jax import lax
from jax.experimental import pallas as pl
from jax.experimental.pallas import tpu as pltpu
from jax.sharding import PartitionSpec as P

VMEM = pl.BlockSpec(memory_space=pltpu.VMEM)
ANY = pl.BlockSpec(memory_space=pl.ANY)
f32 = jnp.float32
bf16 = jnp.bfloat16


def times_root(value, turn, points, sign):
    re, im = value
    turn = turn % points
    if turn == 0:
        return value
    if 4 * turn == points:
        return (-im, re) if sign > 0 else (im, -re)
    if 2 * turn == points:
        return (-re, -im)
    if 4 * turn == 3 * points:
        return (im, -re) if sign > 0 else (-im, re)
    angle = 2.0 * math.pi * turn / points
    c, s = math.cos(angle), sign * math.sin(angle)
    if 8 * turn % points == 0:
        unit = abs(c)
        a = re if c > 0 else -re
        b = im if c > 0 else -im
        if (s > 0) == (c > 0):
            return ((a - b) * unit, (a + b) * unit)
        return ((a + b) * unit, (b - a) * unit)
    return (re * c - im * s, re * s + im * c)


def fourier(values, sign):
    points = len(values)
    if points == 1:
        return values
    if points % 2:
        out = []
        for k in range(points):
            total = values[0]
            for n in range(1, points):
                term = times_root(values[n], k * n, points, sign)
                total = (total[0] + term[0], total[1] + term[1])
            out.append(total)
        return out
    even = fourier(values[0::2], sign)
    odd = fourier(values[1::2], sign)
    low, high = [], []
    for k in range(points // 2):
        a = even[k]
        b = times_root(odd[k], k, points, sign)
        low.append((a[0] + b[0], a[1] + b[1]))
        high.append((a[0] - b[0], a[1] - b[1]))
    return low + high


def tiles_of(cells, rows, lanes):
    step_rows = 8 if rows % 8 == 0 else rows
    step_lanes = 128 if lanes % 128 == 0 else lanes
    return [
        (c, pl.ds(r, step_rows), pl.ds(b, step_lanes))
        for c in range(cells)
        for r in range(0, rows, step_rows)
        for b in range(0, lanes, step_lanes)
    ]


def polarize_kernel(scaling, entries, lesser_hat, polar_hat):
    points, _, cells, rows, lanes = entries.shape
    for c, r, b in tiles_of(cells, rows, lanes):
        hats = []
        for pair in (0, 2):
            hats.append(
                fourier([(entries[n, pair, c, r, b], entries[n, pair + 1, c, r, b]) for n in range(points)], -1)
            )
            if pair == 0:
                for k in range(points):
                    lesser_hat[k, 0, c, r, b] = hats[0][k][0]
                    lesser_hat[k, 1, c, r, b] = hats[0][k][1]
        for k in range(points):
            greater_re, greater_im = hats[1][k]
            lesser_re = lesser_hat[k, 0, c, r, b]
            lesser_im = lesser_hat[k, 1, c, r, b]
            polar_hat[k, 0, c, r, b] = (lesser_re * greater_im - lesser_im * greater_re) * scaling
            polar_hat[k, 1, c, r, b] = (lesser_re * greater_re + lesser_im * greater_im) * scaling


def convolve_kernel(factor, lesser_hat, screened_hat, sigma):
    points, _, cells, rows, lanes = screened_hat.shape
    for c, r, b in tiles_of(cells, rows, lanes):
        spectral = []
        for k in range(points):
            lesser_re, lesser_im = lesser_hat[k, 0, c, r, b], lesser_hat[k, 1, c, r, b]
            w_re, w_im = screened_hat[k, 0, c, r, b], screened_hat[k, 1, c, r, b]
            spectral.append(
                ((lesser_re * w_re - lesser_im * w_im) * factor, (lesser_re * w_im + lesser_im * w_re) * factor)
            )
        for n, (re, im) in enumerate(fourier(spectral, 1)):
            sigma[n, 0, c, r, b] = -im
            sigma[n, 1, c, r, b] = re


def parts(matrix):
    high = matrix.astype(bf16)
    return (high, (matrix - high.astype(f32)).astype(bf16))


def join(pieces, axis):
    return tuple(jnp.concatenate(p, axis) for p in zip(*pieces, strict=True))


def negative(pair):
    return tuple(-p for p in pair)


def product(left, right, turned=False):
    dims = (((1,), (1 if turned else 0,)), ((), ()))
    dot = functools.partial(lax.dot_general, dimension_numbers=dims, preferred_element_type=f32)
    return dot(left[0], right[0]) + (dot(left[0], right[1]) + dot(left[1], right[0]))


def block_of(ref, plane, cell):
    slabs, _, _, rows, lanes = ref.shape
    return ref[:, plane, cell].reshape(slabs * rows, lanes)


def local_terms(cells):
    terms = [(c, c, c) for c in range(cells)]
    for c in range(cells - 1):
        terms.append((c, c + 1, cells + 2 * c))
        terms.append((c + 1, c, cells + 2 * c + 1))
    return sorted(terms)


def matrices_kernel(cells, halos, place, *refs):
    c_diag, c_upper, r_diag, r_upper, c_edge, r_edge = refs[:6]
    c_high, c_low, r_high, r_low = refs[6:]

    def store(ref, i, matrix):
        for out, part in zip(ref, parts(matrix), strict=True):
            out[i] = part

    def fill(refs, read_diag, read_upper, edge):
        for c in range(cells):
            store(refs, c, read_diag(c))
        for c in range(cells - 1):
            store(refs, cells + 2 * c, read_upper(c))
            store(refs, cells + 2 * c + 1, read_upper(c).T)
        first = 3 * cells - 2
        if halos == 1:
            store(refs, first, jnp.where(place[1] == 0, read_upper(cells - 1), edge.T))
        if halos == 2:
            store(refs, first, edge.T)
            store(refs, first + 1, read_upper(cells - 1))

    fill((c_high, c_low), lambda c: (c_diag[c] + c_diag[c].T) * 0.5, lambda c: c_upper[c], c_edge[...])
    for p in range(2):
        fill(
            (r_high.at[p], r_low.at[p]),
            lambda c, p=p: r_diag[p, 0, c],
            lambda c, p=p: r_upper[p, 0, c],
            r_edge[p],
        )


def real_terms(high, low, terms, read, planes):
    lefts, inners = [], []
    for source, i in terms:
        left = (high[i], low[i])
        stacked = parts(jnp.concatenate([read(p, source) for p in range(planes)], 0))
        lefts.append(left)
        inners.append(parts(product(stacked, left, True)))
    left = join(lefts, 1)
    lanes = high.shape[-1]
    return [
        product(left, join([tuple(q[p * lanes : (p + 1) * lanes] for q in i) for i in inners], 0))
        for p in range(planes)
    ]


def complex_terms(high, low, terms, read):
    out_re, out_im = None, None
    for source, i in terms:
        re, im = ((high[p, i], low[p, i]) for p in range(2))
        whole_re, whole_im = (sum(q.astype(f32) for q in pair) for pair in (re, im))
        both, apart = parts(whole_re + whole_im), parts(whole_re - whole_im)
        x_re, x_im = read(0, source), read(1, source)
        a, b = product(re, parts(x_re)), product(im, parts(x_im))
        c = product(both, parts(x_re + x_im))
        t_re, t_im = a - b, c - a - b
        a, b = product(parts(t_re), re, True), product(parts(t_im), im, True)
        c = product(parts(t_re + t_im), apart, True)
        out_re = a + b if out_re is None else out_re + (a + b)
        out_im = c - a + b if out_im is None else out_im + (c - a + b)
    return out_re, out_im


def screen_kernel(here, high, low, out):
    slabs, planes, cells, rows, lanes = here.shape
    for c in range(cells):
        terms = [(source, i) for target, source, i in local_terms(cells) if target == c]
        sums = real_terms(high, low, terms, lambda p, source: block_of(here, p, source), planes)
        for p, total in enumerate(sums):
            out[:, p, c] = total.reshape(slabs, rows, lanes)


def screen_halo_kernel(halos, place, before, *refs):
    received, high, low, out = refs[:halos], refs[halos], refs[halos + 1], refs[halos + 2]
    slabs, planes, cells, rows, lanes = out.shape
    for h in range(halos):
        terms = [(0, 3 * cells - 2 + h)]
        sums = real_terms(high, low, terms, lambda p, source, h=h: block_of(received[h], p, source), planes)
        c = place[2 + h]
        for p, total in enumerate(sums):
            out[:, p, c] = before[:, p, c] + total.reshape(slabs, rows, lanes)


def output_kernel(here, high, low, out):
    cells = here.shape[2]
    for c in range(cells):
        terms = [(source, i) for target, source, i in local_terms(cells) if target == c]
        out[0, 0, c], out[1, 0, c] = complex_terms(high, low, terms, lambda p, source: block_of(here, p, source))


def output_halo_kernel(halos, place, before, *refs):
    received, high, low, out = refs[:halos], refs[halos], refs[halos + 1], refs[halos + 2]
    total, sems = refs[halos + 3 :]
    cells = out.shape[2]

    def touched(c):
        return functools.reduce(jnp.logical_or, [place[2 + h] == c for h in range(halos)])

    def copy_of(ref, c, i):
        return pltpu.make_async_copy(ref, out.at[:, :, c], sems.at[i])

    for c in range(cells):

        @pl.when(jnp.logical_not(touched(c)))
        def _(c=c):
            copy_of(before.at[:, :, c], c, c).start()

    for h in range(halos):
        terms = [(0, 3 * cells - 2 + h)]
        sums = complex_terms(high, low, terms, lambda p, source, h=h: block_of(received[h], p, source))
        c = place[2 + h]
        for p in range(2):
            total[h, p, 0] = before[p, 0, c] + sums[p]
        copy_of(total.at[h], c, cells + h).start()
    for c in range(cells):

        @pl.when(jnp.logical_not(touched(c)))
        def _(c=c):
            copy_of(before.at[:, :, c], c, c).wait()

    for h in range(halos):
        copy_of(total.at[h], place[2 + h], cells + h).wait()


def slabs_kernel(green, slabs, stage, sems_in, sems_out):
    devices, planes, cells, rows, lanes = slabs.shape
    blocks = [(p, c) for p in range(planes) for c in range(cells)]
    into = [
        pltpu.make_async_copy(green.at[p, 0, c].reshape(devices, rows, lanes), stage.at[i], sems_in.at[i])
        for i, (p, c) in enumerate(blocks)
    ]
    out = [pltpu.make_async_copy(stage.at[i], slabs.at[:, p, c], sems_out.at[i]) for i, (p, c) in enumerate(blocks)]
    for copy in into:
        copy.start()
    for first, second in zip(into, out, strict=True):
        first.wait()
        second.start()
    for copy in out:
        copy.wait()


def call(kernel, outs, *args, scalars=False, out_specs=None, **more):
    first = [pl.BlockSpec(memory_space=pltpu.SMEM)] if scalars else []
    return pl.pallas_call(
        kernel,
        out_shape=outs,
        in_specs=first + [VMEM] * (len(args) - len(first)),
        out_specs=out_specs or jax.tree.map(lambda _: VMEM, outs),
        compiler_params=pltpu.CompilerParams(vmem_limit_bytes=16 * 1024 * 1024),
        **more,
    )(*args)


def shape(dims):
    return jax.ShapeDtypeStruct(tuple(dims), f32)


def exchange(values):
    return lax.all_to_all(values, "energy", split_axis=0, concat_axis=0, tiled=True)


def shifted(block, axis, step):
    count = lax.axis_size(axis)
    route = [(i, i + step) for i in range(count) if 0 <= i + step < count]
    return lax.ppermute(block, axis, route)


def swapped(block):
    return lax.ppermute(block, "cell", [(0, 1), (1, 0)])


def halo(values):
    count = lax.axis_size("cell")
    if count == 1:
        return []
    head, tail = values[:, :, :1], values[:, :, -1:]
    if count == 2:
        return [swapped(jnp.where(lax.axis_index("cell") == 0, tail, head))]
    return [shifted(tail, "cell", 1), shifted(head, "cell", -1)]


def place_of(cells):
    count, index = lax.axis_size("cell"), lax.axis_index("cell")
    if count == 1:
        targets = []
    elif count == 2:
        targets = [jnp.where(index == 0, cells - 1, 0)]
    else:
        targets = [0, cells - 1]
    return len(targets), jnp.stack([jnp.asarray(v, jnp.int32) for v in [len(targets), index, *targets]])


def per_device(green_pair, retarded_diag, retarded_upper, coulomb_diag, coulomb_upper):
    devices = lax.axis_size("energy")
    _, held, cells, orbitals, _ = green_pair.shape
    points = devices * held
    scaling = 1.0 / math.sqrt(points)
    rows = orbitals // devices
    halos, place = place_of(cells)
    count = 3 * cells - 2 + halos
    part = jax.ShapeDtypeStruct((count, orbitals, orbitals), bf16)
    pair = jax.ShapeDtypeStruct((2, count, orbitals, orbitals), bf16)
    matrices = call(
        functools.partial(matrices_kernel, cells, halos),
        (part, part, pair, pair),
        place,
        coulomb_diag,
        coulomb_upper,
        retarded_diag,
        retarded_upper,
        shifted(coulomb_upper[-1], "cell", 1),
        shifted(retarded_upper[:, 0, -1], "cell", 1),
        scalars=True,
        cost_estimate=pl.CostEstimate(flops=10**9, bytes_accessed=16 * count * orbitals**2 * 4, transcendentals=0),
    )
    slabs = pl.pallas_call(
        slabs_kernel,
        out_shape=shape((devices, 4, cells, rows, orbitals)),
        in_specs=[ANY],
        out_specs=ANY,
        scratch_shapes=[
            pltpu.VMEM((4 * cells, devices, rows, orbitals), f32),
            pltpu.SemaphoreType.DMA((4 * cells,)),
            pltpu.SemaphoreType.DMA((4 * cells,)),
        ],
    )(green_pair)
    entries, matrices = lax.optimization_barrier((exchange(slabs), matrices))
    coulomb, retarded = matrices[:2], matrices[2:]
    half = shape((points, 2, cells, rows, orbitals))
    lesser_hat, polar_hat = call(functools.partial(polarize_kernel, scaling), (half, half), entries)
    polar = exchange(polar_hat)
    received = halo(polar)
    screened = call(screen_kernel, half, polar, *coulomb)
    if halos:
        screened = call(
            functools.partial(screen_halo_kernel, halos),
            half,
            place,
            screened,
            *received,
            *coulomb,
            scalars=True,
            input_output_aliases={1: 0},
        )
    screened_hat = exchange(screened)
    sigma = exchange(call(functools.partial(convolve_kernel, scaling / points), half, lesser_hat, screened_hat))
    received = halo(sigma)
    out = call(output_kernel, shape(retarded_diag.shape), sigma, *retarded)
    if halos:
        out = call(
            functools.partial(output_halo_kernel, halos),
            shape(out.shape),
            place,
            out,
            *received,
            *retarded,
            scalars=True,
            out_specs=ANY,
            scratch_shapes=[
                pltpu.VMEM((halos, 2, 1, orbitals, orbitals), f32),
                pltpu.SemaphoreType.DMA((cells + halos,)),
            ],
        )
    return out


def solution(mesh):
    over_both = P(None, "energy", "cell", None, None)
    over_cell = P("cell", None, None)
    return jax.shard_map(
        per_device,
        mesh=mesh,
        in_specs=(over_both, over_both, over_both, over_cell, over_cell),
        out_specs=over_both,
        check_vma=False,
    )
```

```python
import functools
import math

import jax
import jax.numpy as jnp
from jax import lax
from jax.experimental import pallas as pl
from jax.experimental.pallas import tpu as pltpu
from jax.sharding import PartitionSpec as P

VMEM = pl.BlockSpec(memory_space=pltpu.VMEM)
ANY = pl.BlockSpec(memory_space=pl.ANY)
f32 = jnp.float32
bf16 = jnp.bfloat16


def times_root(value, turn, points, sign):
    re, im = value
    turn = turn % points
    if turn == 0:
        return value
    if 4 * turn == points:
        return (-im, re) if sign > 0 else (im, -re)
    if 2 * turn == points:
        return (-re, -im)
    if 4 * turn == 3 * points:
        return (im, -re) if sign > 0 else (-im, re)
    angle = 2.0 * math.pi * turn / points
    c, s = math.cos(angle), sign * math.sin(angle)
    if 8 * turn % points == 0:
        unit = abs(c)
        a = re if c > 0 else -re
        b = im if c > 0 else -im
        if (s > 0) == (c > 0):
            return ((a - b) * unit, (a + b) * unit)
        return ((a + b) * unit, (b - a) * unit)
    return (re * c - im * s, re * s + im * c)


def fourier(values, sign):
    points = len(values)
    if points == 1:
        return values
    if points % 2:
        out = []
        for k in range(points):
            total = values[0]
            for n in range(1, points):
                term = times_root(values[n], k * n, points, sign)
                total = (total[0] + term[0], total[1] + term[1])
            out.append(total)
        return out
    even = fourier(values[0::2], sign)
    odd = fourier(values[1::2], sign)
    low, high = [], []
    for k in range(points // 2):
        a = even[k]
        b = times_root(odd[k], k, points, sign)
        low.append((a[0] + b[0], a[1] + b[1]))
        high.append((a[0] - b[0], a[1] - b[1]))
    return low + high


def tiles_of(cells, rows, lanes):
    step_rows = 8 if rows % 8 == 0 else rows
    step_lanes = 128 if lanes % 128 == 0 else lanes
    return [
        (c, pl.ds(r, step_rows), pl.ds(b, step_lanes))
        for c in range(cells)
        for r in range(0, rows, step_rows)
        for b in range(0, lanes, step_lanes)
    ]


def polarize_kernel(scaling, entries, lesser_hat, polar_hat):
    points, _, cells, rows, lanes = entries.shape
    at = places_of(points)
    for c, r, b in tiles_of(cells, rows, lanes):
        hats = []
        for pair in (0, 2):
            hats.append(fourier([(entries[i, pair, c, r, b], entries[i, pair + 1, c, r, b]) for i in at], -1))
            if pair == 0:
                for k in range(points):
                    lesser_hat[k, 0, c, r, b] = hats[0][k][0]
                    lesser_hat[k, 1, c, r, b] = hats[0][k][1]
        for k in range(points):
            greater_re, greater_im = hats[1][k]
            lesser_re = lesser_hat[k, 0, c, r, b]
            lesser_im = lesser_hat[k, 1, c, r, b]
            polar_hat[at[k], 0, c, r, b] = (lesser_re * greater_im - lesser_im * greater_re) * scaling
            polar_hat[at[k], 1, c, r, b] = (lesser_re * greater_re + lesser_im * greater_im) * scaling


def convolve_kernel(factor, lesser_hat, screened_hat, sigma):
    points, _, cells, rows, lanes = screened_hat.shape
    at = places_of(points)
    for c, r, b in tiles_of(cells, rows, lanes):
        spectral = []
        for k in range(points):
            lesser_re, lesser_im = lesser_hat[k, 0, c, r, b], lesser_hat[k, 1, c, r, b]
            w_re, w_im = screened_hat[at[k], 0, c, r, b], screened_hat[at[k], 1, c, r, b]
            spectral.append(
                ((lesser_re * w_re - lesser_im * w_im) * factor, (lesser_re * w_im + lesser_im * w_re) * factor)
            )
        for n, (re, im) in enumerate(fourier(spectral, 1)):
            sigma[at[n], 0, c, r, b] = -im
            sigma[at[n], 1, c, r, b] = re


def parts(matrix):
    high = matrix.astype(bf16)
    return (high, (matrix - high.astype(f32)).astype(bf16))


def join(pieces, axis):
    return tuple(jnp.concatenate(p, axis) for p in zip(*pieces, strict=True))


def negative(pair):
    return tuple(-p for p in pair)


def product(left, right, turned=False):
    dims = (((1,), (1 if turned else 0,)), ((), ()))
    dot = functools.partial(lax.dot_general, dimension_numbers=dims, preferred_element_type=f32)
    return dot(left[0], right[0]) + (dot(left[0], right[1]) + dot(left[1], right[0]))


def block_of(ref, plane, cell):
    slabs, _, _, rows, lanes = ref.shape
    return ref[:, plane, cell].reshape(slabs * rows, lanes)


def local_terms(cells):
    terms = [(c, c, c) for c in range(cells)]
    for c in range(cells - 1):
        terms.append((c, c + 1, cells + 2 * c))
        terms.append((c + 1, c, cells + 2 * c + 1))
    return sorted(terms)


def matrices_kernel(cells, halos, place, *refs):
    c_diag, c_upper, r_diag, r_upper, c_edge, r_edge = refs[:6]
    c_high, c_low, r_high, r_low = refs[6:]

    def store(ref, i, matrix):
        for out, part in zip(ref, parts(matrix), strict=True):
            out[i] = part

    def fill(refs, read_diag, read_upper, edge):
        for c in range(cells):
            store(refs, c, read_diag(c))
        for c in range(cells - 1):
            store(refs, cells + 2 * c, read_upper(c))
            store(refs, cells + 2 * c + 1, read_upper(c).T)
        first = 3 * cells - 2
        if halos == 1:
            store(refs, first, jnp.where(place[1] == 0, read_upper(cells - 1), edge.T))
        if halos == 2:
            store(refs, first, edge.T)
            store(refs, first + 1, read_upper(cells - 1))

    fill((c_high, c_low), lambda c: (c_diag[c] + c_diag[c].T) * 0.5, lambda c: c_upper[c], c_edge[...])
    for p in range(2):
        fill(
            (r_high.at[p], r_low.at[p]),
            lambda c, p=p: r_diag[p, 0, c],
            lambda c, p=p: r_upper[p, 0, c],
            r_edge[p],
        )


def real_terms(high, low, terms, read, planes):
    lefts, inners = [], []
    for source, i in terms:
        left = (high[i], low[i])
        stacked = parts(jnp.concatenate([read(p, source) for p in range(planes)], 0))
        lefts.append(left)
        inners.append(parts(product(stacked, left, True)))
    left = join(lefts, 1)
    lanes = high.shape[-1]
    return [
        product(left, join([tuple(q[p * lanes : (p + 1) * lanes] for q in i) for i in inners], 0))
        for p in range(planes)
    ]


def complex_terms(high, low, terms, read):
    out_re, out_im = None, None
    for source, i in terms:
        re, im = ((high[p, i], low[p, i]) for p in range(2))
        whole_re, whole_im = (sum(q.astype(f32) for q in pair) for pair in (re, im))
        both, apart = parts(whole_re + whole_im), parts(whole_re - whole_im)
        x_re, x_im = read(0, source), read(1, source)
        a, b = product(re, parts(x_re)), product(im, parts(x_im))
        c = product(both, parts(x_re + x_im))
        t_re, t_im = a - b, c - a - b
        a, b = product(parts(t_re), re, True), product(parts(t_im), im, True)
        c = product(parts(t_re + t_im), apart, True)
        out_re = a + b if out_re is None else out_re + (a + b)
        out_im = c - a + b if out_im is None else out_im + (c - a + b)
    return out_re, out_im


def screen_kernel(here, high, low, out):
    slabs, planes, cells, rows, lanes = here.shape
    for c in range(cells):
        terms = [(source, i) for target, source, i in local_terms(cells) if target == c]
        sums = real_terms(high, low, terms, lambda p, source: block_of(here, p, source), planes)
        for p, total in enumerate(sums):
            out[:, p, c] = total.reshape(slabs, rows, lanes)


def screen_halo_kernel(halos, place, before, *refs):
    received, high, low, out = refs[:halos], refs[halos], refs[halos + 1], refs[halos + 2]
    slabs, planes, cells, rows, lanes = out.shape
    for h in range(halos):
        terms = [(0, 3 * cells - 2 + h)]
        sums = real_terms(high, low, terms, lambda p, source, h=h: block_of(received[h], p, source), planes)
        c = place[2 + h]
        for p, total in enumerate(sums):
            out[:, p, c] = before[:, p, c] + total.reshape(slabs, rows, lanes)


def output_kernel(here, high, low, out):
    cells = here.shape[2]
    for c in range(cells):
        terms = [(source, i) for target, source, i in local_terms(cells) if target == c]
        out[0, 0, c], out[1, 0, c] = complex_terms(high, low, terms, lambda p, source: block_of(here, p, source))


def output_halo_kernel(halos, place, before, *refs):
    received, high, low, out = refs[:halos], refs[halos], refs[halos + 1], refs[halos + 2]
    total, sems = refs[halos + 3 :]
    cells = out.shape[2]

    def touched(c):
        return functools.reduce(jnp.logical_or, [place[2 + h] == c for h in range(halos)])

    def copy_of(ref, c, i):
        return pltpu.make_async_copy(ref, out.at[:, :, c], sems.at[i])

    for c in range(cells):

        @pl.when(jnp.logical_not(touched(c)))
        def _(c=c):
            copy_of(before.at[:, :, c], c, c).start()

    for h in range(halos):
        terms = [(0, 3 * cells - 2 + h)]
        sums = complex_terms(high, low, terms, lambda p, source, h=h: block_of(received[h], p, source))
        c = place[2 + h]
        for p in range(2):
            total[h, p, 0] = before[p, 0, c] + sums[p]
        copy_of(total.at[h], c, cells + h).start()
    for c in range(cells):

        @pl.when(jnp.logical_not(touched(c)))
        def _(c=c):
            copy_of(before.at[:, :, c], c, c).wait()

    for h in range(halos):
        copy_of(total.at[h], place[2 + h], cells + h).wait()


def slabs_kernel(green, slabs, stage, sems_in, sems_out):
    devices, planes, cells, rows, lanes = slabs.shape
    blocks = [(p, c) for p in range(planes) for c in range(cells)]
    into = [
        pltpu.make_async_copy(green.at[p, 0, c].reshape(devices, rows, lanes), stage.at[i], sems_in.at[i])
        for i, (p, c) in enumerate(blocks)
    ]
    out = [pltpu.make_async_copy(stage.at[i], slabs.at[:, p, c], sems_out.at[i]) for i, (p, c) in enumerate(blocks)]
    for copy in into:
        copy.start()
    for first, second in zip(into, out, strict=True):
        first.wait()
        second.start()
    for copy in out:
        copy.wait()


def call(kernel, outs, *args, scalars=False, out_specs=None, **more):
    first = [pl.BlockSpec(memory_space=pltpu.SMEM)] if scalars else []
    return pl.pallas_call(
        kernel,
        out_shape=outs,
        in_specs=first + [VMEM] * (len(args) - len(first)),
        out_specs=out_specs or jax.tree.map(lambda _: VMEM, outs),
        compiler_params=pltpu.CompilerParams(vmem_limit_bytes=16 * 1024 * 1024),
        **more,
    )(*args)


def shape(dims):
    return jax.ShapeDtypeStruct(tuple(dims), f32)


def order_of(devices):
    middle = devices // 2
    ends = [e for i in range((devices + 1) // 2) for e in sorted({i, devices - 1 - i})]
    return [middle] + [e for e in ends if e != middle]


def places_of(points):
    order = order_of(points)
    return [order.index(e) for e in range(points)]


def exchange(values):
    order = order_of(lax.axis_size("energy"))
    return lax.all_to_all(
        values, "energy", split_axis=0, concat_axis=0, axis_index_groups=[order], tiled=True
    )


def shifted(block, axis, step):
    count = lax.axis_size(axis)
    route = [(i, i + step) for i in range(count) if 0 <= i + step < count]
    return lax.ppermute(block, axis, route)


def swapped(block):
    return lax.ppermute(block, "cell", [(0, 1), (1, 0)])


def halo(values):
    count = lax.axis_size("cell")
    if count == 1:
        return []
    head, tail = values[:, :, :1], values[:, :, -1:]
    if count == 2:
        return [swapped(jnp.where(lax.axis_index("cell") == 0, tail, head))]
    return [shifted(tail, "cell", 1), shifted(head, "cell", -1)]


def place_of(cells):
    count, index = lax.axis_size("cell"), lax.axis_index("cell")
    if count == 1:
        targets = []
    elif count == 2:
        targets = [jnp.where(index == 0, cells - 1, 0)]
    else:
        targets = [0, cells - 1]
    return len(targets), jnp.stack([jnp.asarray(v, jnp.int32) for v in [len(targets), index, *targets]])


def per_device(green_pair, retarded_diag, retarded_upper, coulomb_diag, coulomb_upper):
    devices = lax.axis_size("energy")
    _, held, cells, orbitals, _ = green_pair.shape
    points = devices * held
    scaling = 1.0 / math.sqrt(points)
    rows = orbitals // devices
    halos, place = place_of(cells)
    count = 3 * cells - 2 + halos
    part = jax.ShapeDtypeStruct((count, orbitals, orbitals), bf16)
    pair = jax.ShapeDtypeStruct((2, count, orbitals, orbitals), bf16)
    matrices = call(
        functools.partial(matrices_kernel, cells, halos),
        (part, part, pair, pair),
        place,
        coulomb_diag,
        coulomb_upper,
        retarded_diag,
        retarded_upper,
        shifted(coulomb_upper[-1], "cell", 1),
        shifted(retarded_upper[:, 0, -1], "cell", 1),
        scalars=True,
        cost_estimate=pl.CostEstimate(flops=10**9, bytes_accessed=16 * count * orbitals**2 * 4, transcendentals=0),
    )
    slabs = pl.pallas_call(
        slabs_kernel,
        out_shape=shape((devices, 4, cells, rows, orbitals)),
        in_specs=[ANY],
        out_specs=ANY,
        scratch_shapes=[
            pltpu.VMEM((4 * cells, devices, rows, orbitals), f32),
            pltpu.SemaphoreType.DMA((4 * cells,)),
            pltpu.SemaphoreType.DMA((4 * cells,)),
        ],
    )(green_pair)
    entries, matrices = lax.optimization_barrier((exchange(slabs), matrices))
    coulomb, retarded = matrices[:2], matrices[2:]
    half = shape((points, 2, cells, rows, orbitals))
    lesser_hat, polar_hat = call(functools.partial(polarize_kernel, scaling), (half, half), entries)
    polar = exchange(polar_hat)
    received = halo(polar)
    screened = call(screen_kernel, half, polar, *coulomb)
    if halos:
        screened = call(
            functools.partial(screen_halo_kernel, halos),
            half,
            place,
            screened,
            *received,
            *coulomb,
            scalars=True,
            input_output_aliases={1: 0},
        )
    screened_hat = exchange(screened)
    sigma = exchange(call(functools.partial(convolve_kernel, scaling / points), half, lesser_hat, screened_hat))
    received = halo(sigma)
    out = call(output_kernel, shape(retarded_diag.shape), sigma, *retarded)
    if halos:
        out = call(
            functools.partial(output_halo_kernel, halos),
            shape(out.shape),
            place,
            out,
            *received,
            *retarded,
            scalars=True,
            out_specs=ANY,
            scratch_shapes=[
                pltpu.VMEM((halos, 2, 1, orbitals, orbitals), f32),
                pltpu.SemaphoreType.DMA((cells + halos,)),
            ],
        )
    return out


def solution(mesh):
    over_both = P(None, "energy", "cell", None, None)
    over_cell = P("cell", None, None)
    return jax.shard_map(
        per_device,
        mesh=mesh,
        in_specs=(over_both, over_both, over_both, over_cell, over_cell),
        out_specs=over_both,
        check_vma=False,
    )
```

```python
import functools
import math

import jax
import jax.numpy as jnp
from jax import lax
from jax.experimental import pallas as pl
from jax.experimental.pallas import tpu as pltpu
from jax.sharding import PartitionSpec as P

VMEM = pl.BlockSpec(memory_space=pltpu.VMEM)
ANY = pl.BlockSpec(memory_space=pl.ANY)
f32 = jnp.float32
bf16 = jnp.bfloat16


def times_root(value, turn, points, sign):
    re, im = value
    turn = turn % points
    if turn == 0:
        return value
    if 4 * turn == points:
        return (-im, re) if sign > 0 else (im, -re)
    if 2 * turn == points:
        return (-re, -im)
    if 4 * turn == 3 * points:
        return (im, -re) if sign > 0 else (-im, re)
    angle = 2.0 * math.pi * turn / points
    c, s = math.cos(angle), sign * math.sin(angle)
    if 8 * turn % points == 0:
        unit = abs(c)
        a = re if c > 0 else -re
        b = im if c > 0 else -im
        if (s > 0) == (c > 0):
            return ((a - b) * unit, (a + b) * unit)
        return ((a + b) * unit, (b - a) * unit)
    return (re * c - im * s, re * s + im * c)


def fourier(values, sign):
    points = len(values)
    if points == 1:
        return values
    if points % 2:
        out = []
        for k in range(points):
            total = values[0]
            for n in range(1, points):
                term = times_root(values[n], k * n, points, sign)
                total = (total[0] + term[0], total[1] + term[1])
            out.append(total)
        return out
    even = fourier(values[0::2], sign)
    odd = fourier(values[1::2], sign)
    low, high = [], []
    for k in range(points // 2):
        a = even[k]
        b = times_root(odd[k], k, points, sign)
        low.append((a[0] + b[0], a[1] + b[1]))
        high.append((a[0] - b[0], a[1] - b[1]))
    return low + high


def tiles_of(cells, rows, lanes):
    step_rows = 8 if rows % 8 == 0 else rows
    step_lanes = 128 if lanes % 128 == 0 else lanes
    return [
        (c, pl.ds(r, step_rows), pl.ds(b, step_lanes))
        for c in range(cells)
        for r in range(0, rows, step_rows)
        for b in range(0, lanes, step_lanes)
    ]


def polarize_kernel(scaling, entries, lesser_hat, polar_hat):
    points, _, cells, rows, lanes = entries.shape
    at = places_of(points)
    for c, r, b in tiles_of(cells, rows, lanes):
        hats = []
        for pair in (0, 2):
            hats.append(fourier([(entries[i, pair, c, r, b], entries[i, pair + 1, c, r, b]) for i in at], -1))
            if pair == 0:
                for k in range(points):
                    lesser_hat[k, 0, c, r, b] = hats[0][k][0]
                    lesser_hat[k, 1, c, r, b] = hats[0][k][1]
        for k in range(points):
            greater_re, greater_im = hats[1][k]
            lesser_re = lesser_hat[k, 0, c, r, b]
            lesser_im = lesser_hat[k, 1, c, r, b]
            polar_hat[at[k], 0, c, r, b] = (lesser_re * greater_im - lesser_im * greater_re) * scaling
            polar_hat[at[k], 1, c, r, b] = (lesser_re * greater_re + lesser_im * greater_im) * scaling


def convolve_kernel(factor, lesser_hat, screened_hat, sigma):
    points, _, cells, rows, lanes = screened_hat.shape
    at = places_of(points)
    for c, r, b in tiles_of(cells, rows, lanes):
        spectral = []
        for k in range(points):
            lesser_re, lesser_im = lesser_hat[k, 0, c, r, b], lesser_hat[k, 1, c, r, b]
            w_re, w_im = screened_hat[at[k], 0, c, r, b], screened_hat[at[k], 1, c, r, b]
            spectral.append(
                ((lesser_re * w_re - lesser_im * w_im) * factor, (lesser_re * w_im + lesser_im * w_re) * factor)
            )
        for n, (re, im) in enumerate(fourier(spectral, 1)):
            sigma[at[n], 0, c, r, b] = -im
            sigma[at[n], 1, c, r, b] = re


def parts(matrix):
    high = matrix.astype(bf16)
    return (high, (matrix - high.astype(f32)).astype(bf16))


def join(pieces, axis):
    return tuple(jnp.concatenate(p, axis) for p in zip(*pieces, strict=True))


def negative(pair):
    return tuple(-p for p in pair)


def product(left, right, turned=False):
    dims = (((1,), (1 if turned else 0,)), ((), ()))
    dot = functools.partial(lax.dot_general, dimension_numbers=dims, preferred_element_type=f32)
    return dot(left[0], right[0]) + (dot(left[0], right[1]) + dot(left[1], right[0]))


def block_of(ref, plane, cell):
    slabs, _, _, rows, lanes = ref.shape
    return ref[:, plane, cell].reshape(slabs * rows, lanes)


def local_terms(cells):
    terms = [(c, c, c) for c in range(cells)]
    for c in range(cells - 1):
        terms.append((c, c + 1, cells + 2 * c))
        terms.append((c + 1, c, cells + 2 * c + 1))
    return sorted(terms)


def matrices_kernel(cells, halos, place, *refs):
    c_diag, c_upper, r_diag, r_upper, c_edge, r_edge = refs[:6]
    c_high, c_low, r_high, r_low = refs[6:]

    def store(ref, i, matrix):
        for out, part in zip(ref, parts(matrix), strict=True):
            out[i] = part

    def fill(refs, read_diag, read_upper, edge):
        for c in range(cells):
            store(refs, c, read_diag(c))
        for c in range(cells - 1):
            store(refs, cells + 2 * c, read_upper(c))
            store(refs, cells + 2 * c + 1, read_upper(c).T)
        first = 3 * cells - 2
        if halos == 1:
            store(refs, first, jnp.where(place[1] == 0, read_upper(cells - 1), edge.T))
        if halos == 2:
            store(refs, first, edge.T)
            store(refs, first + 1, read_upper(cells - 1))

    fill((c_high, c_low), lambda c: (c_diag[c] + c_diag[c].T) * 0.5, lambda c: c_upper[c], c_edge[...])
    for p in range(2):
        fill(
            (r_high.at[p], r_low.at[p]),
            lambda c, p=p: r_diag[p, 0, c],
            lambda c, p=p: r_upper[p, 0, c],
            r_edge[p],
        )


def real_terms(high, low, terms, read, planes):
    lefts, inners = [], []
    for source, i in terms:
        left = (high[i], low[i])
        stacked = parts(jnp.concatenate([read(p, source) for p in range(planes)], 0))
        lefts.append(left)
        inners.append(parts(product(stacked, left, True)))
    left = join(lefts, 1)
    lanes = high.shape[-1]
    return [
        product(left, join([tuple(q[p * lanes : (p + 1) * lanes] for q in i) for i in inners], 0))
        for p in range(planes)
    ]


def complex_terms(high, low, terms, read):
    out_re, out_im = None, None
    for source, i in terms:
        re, im = ((high[p, i], low[p, i]) for p in range(2))
        whole_re, whole_im = (sum(q.astype(f32) for q in pair) for pair in (re, im))
        both, apart = parts(whole_re + whole_im), parts(whole_re - whole_im)
        x_re, x_im = read(0, source), read(1, source)
        a, b = product(re, parts(x_re)), product(im, parts(x_im))
        c = product(both, parts(x_re + x_im))
        t_re, t_im = a - b, c - a - b
        a, b = product(parts(t_re), re, True), product(parts(t_im), im, True)
        c = product(parts(t_re + t_im), apart, True)
        out_re = a + b if out_re is None else out_re + (a + b)
        out_im = c - a + b if out_im is None else out_im + (c - a + b)
    return out_re, out_im


def real_term(left, blocks):
    lanes = left[0].shape[-1]
    first = parts(product(left, parts(jnp.concatenate(blocks, 1))))
    count = len(blocks)
    stacked = tuple(jnp.concatenate([q[:, p * lanes : (p + 1) * lanes] for p in range(count)], 0) for q in first)
    total = product(stacked, left, True)
    return [total[p * lanes : (p + 1) * lanes] for p in range(count)]


def screen_kernel(here, high, low, out):
    slabs, planes, cells, rows, lanes = here.shape
    for c in range(cells):
        terms = [(source, i) for target, source, i in local_terms(cells) if target == c]
        sums = real_terms(high, low, terms, lambda p, source: block_of(here, p, source), planes)
        for p, total in enumerate(sums):
            out[:, p, c] = total.reshape(slabs, rows, lanes)


def screen_halo_kernel(halos, place, before, *refs):
    received, high, low, out = refs[:halos], refs[halos], refs[halos + 1], refs[halos + 2]
    slabs, planes, cells, rows, lanes = out.shape
    for h in range(halos):
        i = 3 * cells - 2 + h
        sums = real_term((high[i], low[i]), [block_of(received[h], p, 0) for p in range(planes)])
        c = place[2 + h]
        for p, total in enumerate(sums):
            out[:, p, c] = before[:, p, c] + total.reshape(slabs, rows, lanes)


def output_kernel(here, high, low, out):
    cells = here.shape[2]
    for c in range(cells):
        terms = [(source, i) for target, source, i in local_terms(cells) if target == c]
        out[0, 0, c], out[1, 0, c] = complex_terms(high, low, terms, lambda p, source: block_of(here, p, source))


def output_halo_kernel(halos, place, before, *refs):
    received, high, low, out = refs[:halos], refs[halos], refs[halos + 1], refs[halos + 2]
    total, sems = refs[halos + 3 :]
    cells = out.shape[2]

    def touched(c):
        return functools.reduce(jnp.logical_or, [place[2 + h] == c for h in range(halos)])

    def copy_of(ref, c, i):
        return pltpu.make_async_copy(ref, out.at[:, :, c], sems.at[i])

    for c in range(cells):

        @pl.when(jnp.logical_not(touched(c)))
        def _(c=c):
            copy_of(before.at[:, :, c], c, c).start()

    for h in range(halos):
        terms = [(0, 3 * cells - 2 + h)]
        sums = complex_terms(high, low, terms, lambda p, source, h=h: block_of(received[h], p, source))
        c = place[2 + h]
        for p in range(2):
            total[h, p, 0] = before[p, 0, c] + sums[p]
        copy_of(total.at[h], c, cells + h).start()
    for c in range(cells):

        @pl.when(jnp.logical_not(touched(c)))
        def _(c=c):
            copy_of(before.at[:, :, c], c, c).wait()

    for h in range(halos):
        copy_of(total.at[h], place[2 + h], cells + h).wait()


def slabs_kernel(green, slabs, stage, sems_in, sems_out):
    devices, planes, cells, rows, lanes = slabs.shape
    blocks = [(p, c) for p in range(planes) for c in range(cells)]
    into = [
        pltpu.make_async_copy(green.at[p, 0, c].reshape(devices, rows, lanes), stage.at[i], sems_in.at[i])
        for i, (p, c) in enumerate(blocks)
    ]
    out = [pltpu.make_async_copy(stage.at[i], slabs.at[:, p, c], sems_out.at[i]) for i, (p, c) in enumerate(blocks)]
    for copy in into:
        copy.start()
    for first, second in zip(into, out, strict=True):
        first.wait()
        second.start()
    for copy in out:
        copy.wait()


def call(kernel, outs, *args, scalars=False, out_specs=None, **more):
    first = [pl.BlockSpec(memory_space=pltpu.SMEM)] if scalars else []
    return pl.pallas_call(
        kernel,
        out_shape=outs,
        in_specs=first + [VMEM] * (len(args) - len(first)),
        out_specs=out_specs or jax.tree.map(lambda _: VMEM, outs),
        compiler_params=pltpu.CompilerParams(vmem_limit_bytes=16 * 1024 * 1024),
        **more,
    )(*args)


def shape(dims):
    return jax.ShapeDtypeStruct(tuple(dims), f32)


def order_of(devices):
    return [(e + devices // 2 + 1) % devices for e in range(devices)]


def places_of(points):
    order = order_of(points)
    return [order.index(e) for e in range(points)]


def exchange(values):
    order = order_of(lax.axis_size("energy"))
    return lax.all_to_all(
        values, "energy", split_axis=0, concat_axis=0, axis_index_groups=[order], tiled=True
    )


def shifted(block, axis, step):
    count = lax.axis_size(axis)
    route = [(i, i + step) for i in range(count) if 0 <= i + step < count]
    return lax.ppermute(block, axis, route)


def swapped(block):
    return lax.ppermute(block, "cell", [(0, 1), (1, 0)])


def halo(values):
    count = lax.axis_size("cell")
    if count == 1:
        return []
    head, tail = values[:, :, :1], values[:, :, -1:]
    if count == 2:
        return [swapped(jnp.where(lax.axis_index("cell") == 0, tail, head))]
    return [shifted(tail, "cell", 1), shifted(head, "cell", -1)]


def place_of(cells):
    count, index = lax.axis_size("cell"), lax.axis_index("cell")
    if count == 1:
        targets = []
    elif count == 2:
        targets = [jnp.where(index == 0, cells - 1, 0)]
    else:
        targets = [0, cells - 1]
    return len(targets), jnp.stack([jnp.asarray(v, jnp.int32) for v in [len(targets), index, *targets]])


def per_device(green_pair, retarded_diag, retarded_upper, coulomb_diag, coulomb_upper):
    devices = lax.axis_size("energy")
    _, held, cells, orbitals, _ = green_pair.shape
    points = devices * held
    scaling = 1.0 / math.sqrt(points)
    rows = orbitals // devices
    halos, place = place_of(cells)
    count = 3 * cells - 2 + halos
    part = jax.ShapeDtypeStruct((count, orbitals, orbitals), bf16)
    pair = jax.ShapeDtypeStruct((2, count, orbitals, orbitals), bf16)
    matrices = call(
        functools.partial(matrices_kernel, cells, halos),
        (part, part, pair, pair),
        place,
        coulomb_diag,
        coulomb_upper,
        retarded_diag,
        retarded_upper,
        shifted(coulomb_upper[-1], "cell", 1),
        shifted(retarded_upper[:, 0, -1], "cell", 1),
        scalars=True,
        cost_estimate=pl.CostEstimate(flops=10**9, bytes_accessed=16 * count * orbitals**2 * 4, transcendentals=0),
    )
    slabs = pl.pallas_call(
        slabs_kernel,
        out_shape=shape((devices, 4, cells, rows, orbitals)),
        in_specs=[ANY],
        out_specs=ANY,
        scratch_shapes=[
            pltpu.VMEM((4 * cells, devices, rows, orbitals), f32),
            pltpu.SemaphoreType.DMA((4 * cells,)),
            pltpu.SemaphoreType.DMA((4 * cells,)),
        ],
    )(green_pair)
    entries, matrices = lax.optimization_barrier((exchange(slabs), matrices))
    coulomb, retarded = matrices[:2], matrices[2:]
    half = shape((points, 2, cells, rows, orbitals))
    lesser_hat, polar_hat = call(functools.partial(polarize_kernel, scaling), (half, half), entries)
    polar = exchange(polar_hat)
    received = halo(polar)
    screened = call(screen_kernel, half, polar, *coulomb)
    if halos:
        screened = call(
            functools.partial(screen_halo_kernel, halos),
            half,
            place,
            screened,
            *received,
            *coulomb,
            scalars=True,
            input_output_aliases={1: 0},
        )
    screened_hat = exchange(screened)
    sigma = exchange(call(functools.partial(convolve_kernel, scaling / points), half, lesser_hat, screened_hat))
    received = halo(sigma)
    out = call(output_kernel, shape(retarded_diag.shape), sigma, *retarded)
    if halos:
        out = call(
            functools.partial(output_halo_kernel, halos),
            shape(out.shape),
            place,
            out,
            *received,
            *retarded,
            scalars=True,
            out_specs=ANY,
            scratch_shapes=[
                pltpu.VMEM((halos, 2, 1, orbitals, orbitals), f32),
                pltpu.SemaphoreType.DMA((cells + halos,)),
            ],
        )
    return out


def solution(mesh):
    over_both = P(None, "energy", "cell", None, None)
    over_cell = P("cell", None, None)
    return jax.shard_map(
        per_device,
        mesh=mesh,
        in_specs=(over_both, over_both, over_both, over_cell, over_cell),
        out_specs=over_both,
        check_vma=False,
    )
```

```python
import functools
import math

import jax
import jax.numpy as jnp
from jax import lax
from jax.experimental import pallas as pl
from jax.experimental.pallas import tpu as pltpu
from jax.sharding import PartitionSpec as P

VMEM = pl.BlockSpec(memory_space=pltpu.VMEM)
ANY = pl.BlockSpec(memory_space=pl.ANY)
f32 = jnp.float32
bf16 = jnp.bfloat16


def times_root(value, turn, points, sign):
    re, im = value
    turn = turn % points
    if turn == 0:
        return value
    if 4 * turn == points:
        return (-im, re) if sign > 0 else (im, -re)
    if 2 * turn == points:
        return (-re, -im)
    if 4 * turn == 3 * points:
        return (im, -re) if sign > 0 else (-im, re)
    angle = 2.0 * math.pi * turn / points
    c, s = math.cos(angle), sign * math.sin(angle)
    if 8 * turn % points == 0:
        unit = abs(c)
        a = re if c > 0 else -re
        b = im if c > 0 else -im
        if (s > 0) == (c > 0):
            return ((a - b) * unit, (a + b) * unit)
        return ((a + b) * unit, (b - a) * unit)
    return (re * c - im * s, re * s + im * c)


def fourier(values, sign):
    points = len(values)
    if points == 1:
        return values
    if points % 2:
        out = []
        for k in range(points):
            total = values[0]
            for n in range(1, points):
                term = times_root(values[n], k * n, points, sign)
                total = (total[0] + term[0], total[1] + term[1])
            out.append(total)
        return out
    even = fourier(values[0::2], sign)
    odd = fourier(values[1::2], sign)
    low, high = [], []
    for k in range(points // 2):
        a = even[k]
        b = times_root(odd[k], k, points, sign)
        low.append((a[0] + b[0], a[1] + b[1]))
        high.append((a[0] - b[0], a[1] - b[1]))
    return low + high


def tiles_of(cells, rows, lanes):
    step_rows = 8 if rows % 8 == 0 else rows
    step_lanes = 128 if lanes % 128 == 0 else lanes
    return [
        (c, pl.ds(r, step_rows), pl.ds(b, step_lanes))
        for c in range(cells)
        for r in range(0, rows, step_rows)
        for b in range(0, lanes, step_lanes)
    ]


def polarize_kernel(scaling, entries, lesser_hat, polar_hat):
    points, _, cells, rows, lanes = entries.shape
    at = places_of(points)
    for c, r, b in tiles_of(cells, rows, lanes):
        hats = []
        for pair in (0, 2):
            hats.append(fourier([(entries[i, pair, c, r, b], entries[i, pair + 1, c, r, b]) for i in at], -1))
            if pair == 0:
                for k in range(points):
                    lesser_hat[k, 0, c, r, b] = hats[0][k][0]
                    lesser_hat[k, 1, c, r, b] = hats[0][k][1]
        for k in range(points):
            greater_re, greater_im = hats[1][k]
            lesser_re = lesser_hat[k, 0, c, r, b]
            lesser_im = lesser_hat[k, 1, c, r, b]
            polar_hat[at[k], 0, c, r, b] = (lesser_re * greater_im - lesser_im * greater_re) * scaling
            polar_hat[at[k], 1, c, r, b] = (lesser_re * greater_re + lesser_im * greater_im) * scaling


def convolve_kernel(factor, lesser_hat, screened_hat, sigma):
    points, _, cells, rows, lanes = screened_hat.shape
    at = places_of(points)
    for c, r, b in tiles_of(cells, rows, lanes):
        spectral = []
        for k in range(points):
            lesser_re, lesser_im = lesser_hat[k, 0, c, r, b], lesser_hat[k, 1, c, r, b]
            w_re, w_im = screened_hat[at[k], 0, c, r, b], screened_hat[at[k], 1, c, r, b]
            spectral.append(
                ((lesser_re * w_re - lesser_im * w_im) * factor, (lesser_re * w_im + lesser_im * w_re) * factor)
            )
        for n, (re, im) in enumerate(fourier(spectral, 1)):
            sigma[at[n], 0, c, r, b] = -im
            sigma[at[n], 1, c, r, b] = re


def parts(matrix):
    high = matrix.astype(bf16)
    return (high, (matrix - high.astype(f32)).astype(bf16))


def join(pieces, axis):
    return tuple(jnp.concatenate(p, axis) for p in zip(*pieces, strict=True))


def negative(pair):
    return tuple(-p for p in pair)


def product(left, right, turned=False):
    dims = (((1,), (1 if turned else 0,)), ((), ()))
    dot = functools.partial(lax.dot_general, dimension_numbers=dims, preferred_element_type=f32)
    return dot(left[0], right[0]) + (dot(left[0], right[1]) + dot(left[1], right[0]))


def block_of(ref, plane, cell):
    slabs, _, _, rows, lanes = ref.shape
    return ref[:, plane, cell].reshape(slabs * rows, lanes)


def local_terms(cells):
    terms = [(c, c, c) for c in range(cells)]
    for c in range(cells - 1):
        terms.append((c, c + 1, cells + 2 * c))
        terms.append((c + 1, c, cells + 2 * c + 1))
    return sorted(terms)


def matrices_kernel(cells, halos, place, *refs):
    c_diag, c_upper, r_diag, r_upper, c_edge, r_edge = refs[:6]
    c_high, c_low, r_high, r_low = refs[6:]

    def store(ref, i, matrix):
        for out, part in zip(ref, parts(matrix), strict=True):
            out[i] = part

    def fill(refs, read_diag, read_upper, edge):
        for c in range(cells):
            store(refs, c, read_diag(c))
        for c in range(cells - 1):
            store(refs, cells + 2 * c, read_upper(c))
            store(refs, cells + 2 * c + 1, read_upper(c).T)
        first = 3 * cells - 2
        if halos == 1:
            store(refs, first, jnp.where(place[1] == 0, read_upper(cells - 1), edge.T))
        if halos == 2:
            store(refs, first, edge.T)
            store(refs, first + 1, read_upper(cells - 1))

    fill((c_high, c_low), lambda c: (c_diag[c] + c_diag[c].T) * 0.5, lambda c: c_upper[c], c_edge[...])
    for p in range(2):
        fill(
            (r_high.at[p], r_low.at[p]),
            lambda c, p=p: r_diag[p, 0, c],
            lambda c, p=p: r_upper[p, 0, c],
            r_edge[p],
        )


def real_terms(high, low, terms, read, planes):
    lefts, inners = [], []
    for source, i in terms:
        left = (high[i], low[i])
        stacked = parts(jnp.concatenate([read(p, source) for p in range(planes)], 0))
        lefts.append(left)
        inners.append(parts(product(stacked, left, True)))
    left = join(lefts, 1)
    lanes = high.shape[-1]
    return [
        product(left, join([tuple(q[p * lanes : (p + 1) * lanes] for q in i) for i in inners], 0))
        for p in range(planes)
    ]


def complex_terms(high, low, terms, read, on_real=None):
    out_re, out_im = None, None
    for source, i in terms:
        re, im = ((high[p, i], low[p, i]) for p in range(2))
        whole_re, whole_im = (sum(q.astype(f32) for q in pair) for pair in (re, im))
        both, apart = parts(whole_re + whole_im), parts(whole_re - whole_im)
        x_re, x_im = read(0, source), read(1, source)
        a, b = product(re, parts(x_re)), product(im, parts(x_im))
        c = product(both, parts(x_re + x_im))
        t_re, t_im = a - b, c - a - b
        a, b = product(parts(t_re), re, True), product(parts(t_im), im, True)
        out_re = a + b if out_re is None else out_re + (a + b)
        if on_real is not None and (source, i) == terms[-1]:
            on_real(out_re)
        c = product(parts(t_re + t_im), apart, True)
        out_im = c - a + b if out_im is None else out_im + (c - a + b)
    return out_re, out_im


def real_term(left, blocks):
    lanes = left[0].shape[-1]
    first = parts(product(left, parts(jnp.concatenate(blocks, 1))))
    count = len(blocks)
    stacked = tuple(jnp.concatenate([q[:, p * lanes : (p + 1) * lanes] for p in range(count)], 0) for q in first)
    total = product(stacked, left, True)
    return [total[p * lanes : (p + 1) * lanes] for p in range(count)]


def screen_kernel(here, high, low, out):
    slabs, planes, cells, rows, lanes = here.shape
    for c in range(cells):
        terms = [(source, i) for target, source, i in local_terms(cells) if target == c]
        sums = real_terms(high, low, terms, lambda p, source: block_of(here, p, source), planes)
        for p, total in enumerate(sums):
            out[:, p, c] = total.reshape(slabs, rows, lanes)


def screen_halo_kernel(halos, place, before, *refs):
    received, high, low, out = refs[:halos], refs[halos], refs[halos + 1], refs[halos + 2]
    slabs, planes, cells, rows, lanes = out.shape
    for c in range(cells):

        @pl.when(untouched(halos, place, c))
        def _(c=c):
            out[:, :, c] = before[:, :, c]

    for h in range(halos):
        i = 3 * cells - 2 + h
        sums = real_term((high[i], low[i]), [block_of(received[h], p, 0) for p in range(planes)])
        c = place[2 + h]
        for p, total in enumerate(sums):
            out[:, p, c] = before[:, p, c] + total.reshape(slabs, rows, lanes)


def untouched(halos, place, c):
    return functools.reduce(jnp.logical_and, [place[2 + h] != c for h in range(halos)])


def output_kernel(here, high, low, out):
    cells = here.shape[2]
    for c in range(cells):
        terms = [(source, i) for target, source, i in local_terms(cells) if target == c]
        out[0, 0, c], out[1, 0, c] = complex_terms(high, low, terms, lambda p, source: block_of(here, p, source))


def output_halo_kernel(halos, place, before, *refs):
    received, high, low, out = refs[:halos], refs[halos], refs[halos + 1], refs[halos + 2]
    total, sems = refs[halos + 3 :]
    cells = out.shape[2]

    def copy_of(ref, p, c, i):
        return pltpu.make_async_copy(ref, out.at[p, 0, c], sems.at[i])

    def kept(c):
        return [copy_of(before.at[p, 0, c], p, c, 2 * c + p) for p in range(2)]

    def added(h):
        return [copy_of(total.at[h, p], p, place[2 + h], 2 * (cells + h) + p) for p in range(2)]

    for c in range(cells):

        @pl.when(untouched(halos, place, c))
        def _(c=c):
            for copy in kept(c):
                copy.start()

    for h in range(halos):
        terms = [(0, 3 * cells - 2 + h)]
        c = place[2 + h]

        def send(p, value, h=h, c=c):
            total[h, p] = before[p, 0, c] + value
            added(h)[p].start()

        sums = complex_terms(
            high,
            low,
            terms,
            lambda p, source, h=h: block_of(received[h], p, source),
            functools.partial(send, 0),
        )
        send(1, sums[1])
    for c in range(cells):

        @pl.when(untouched(halos, place, c))
        def _(c=c):
            for copy in kept(c):
                copy.wait()

    for h in range(halos):
        for copy in added(h):
            copy.wait()


def slabs_kernel(green, slabs, stage, sems_in, sems_out):
    devices, planes, cells, rows, lanes = slabs.shape
    blocks = [(p, c) for p in range(planes) for c in range(cells)]
    into = [
        pltpu.make_async_copy(green.at[p, 0, c], stage.at[i], sems_in.at[i])
        for i, (p, c) in enumerate(blocks)
    ]
    out = [pltpu.make_async_copy(stage.at[i], slabs.at[:, p, c], sems_out.at[i]) for i, (p, c) in enumerate(blocks)]
    for copy in into:
        copy.start()
    for first, second in zip(into, out, strict=True):
        first.wait()
        second.start()
    for copy in out:
        copy.wait()


def call(kernel, outs, *args, scalars=False, out_specs=None, **more):
    first = [pl.BlockSpec(memory_space=pltpu.SMEM)] if scalars else []
    return pl.pallas_call(
        kernel,
        out_shape=outs,
        in_specs=first + [VMEM] * (len(args) - len(first)),
        out_specs=out_specs or jax.tree.map(lambda _: VMEM, outs),
        compiler_params=pltpu.CompilerParams(vmem_limit_bytes=16 * 1024 * 1024),
        **more,
    )(*args)


def shape(dims):
    return jax.ShapeDtypeStruct(tuple(dims), f32)


def order_of(devices):
    return [(e + devices // 2 + 1) % devices for e in range(devices)]


def places_of(points):
    order = order_of(points)
    return [order.index(e) for e in range(points)]


def exchange(values):
    order = order_of(lax.axis_size("energy"))
    return lax.all_to_all(
        values, "energy", split_axis=0, concat_axis=0, axis_index_groups=[order], tiled=True
    )


def shifted(block, axis, step):
    count = lax.axis_size(axis)
    route = [(i, i + step) for i in range(count) if 0 <= i + step < count]
    return lax.ppermute(block, axis, route)


def swapped(block):
    return lax.ppermute(block, "cell", [(0, 1), (1, 0)])


def halo(values):
    count = lax.axis_size("cell")
    if count == 1:
        return []
    head, tail = values[:, :, :1], values[:, :, -1:]
    if count == 2:
        return [swapped(jnp.where(lax.axis_index("cell") == 0, tail, head))]
    return [shifted(tail, "cell", 1), shifted(head, "cell", -1)]


def place_of(cells):
    count, index = lax.axis_size("cell"), lax.axis_index("cell")
    if count == 1:
        targets = []
    elif count == 2:
        targets = [jnp.where(index == 0, cells - 1, 0)]
    else:
        targets = [0, cells - 1]
    return len(targets), jnp.stack([jnp.asarray(v, jnp.int32) for v in [len(targets), index, *targets]])


def per_device(green_pair, retarded_diag, retarded_upper, coulomb_diag, coulomb_upper):
    devices = lax.axis_size("energy")
    _, held, cells, orbitals, _ = green_pair.shape
    points = devices * held
    scaling = 1.0 / math.sqrt(points)
    rows = orbitals // devices
    halos, place = place_of(cells)
    count = 3 * cells - 2 + halos
    part = jax.ShapeDtypeStruct((count, orbitals, orbitals), bf16)
    pair = jax.ShapeDtypeStruct((2, count, orbitals, orbitals), bf16)
    matrices = call(
        functools.partial(matrices_kernel, cells, halos),
        (part, part, pair, pair),
        place,
        coulomb_diag,
        coulomb_upper,
        retarded_diag,
        retarded_upper,
        shifted(coulomb_upper[-1], "cell", 1),
        shifted(retarded_upper[:, 0, -1], "cell", 1),
        scalars=True,
        cost_estimate=pl.CostEstimate(flops=10**9, bytes_accessed=16 * count * orbitals**2 * 4, transcendentals=0),
    )
    slabs = pl.pallas_call(
        slabs_kernel,
        out_shape=shape((devices, 4, cells, rows, orbitals)),
        in_specs=[ANY],
        out_specs=ANY,
        scratch_shapes=[
            pltpu.VMEM((4 * cells, devices, rows, orbitals), f32),
            pltpu.SemaphoreType.DMA((4 * cells,)),
            pltpu.SemaphoreType.DMA((4 * cells,)),
        ],
    )(green_pair.reshape(4, held, cells, devices, rows, orbitals))
    entries, matrices = lax.optimization_barrier((exchange(slabs), matrices))
    coulomb, retarded = matrices[:2], matrices[2:]
    half = shape((points, 2, cells, rows, orbitals))
    lesser_hat, polar_hat = call(functools.partial(polarize_kernel, scaling), (half, half), entries)
    polar = exchange(polar_hat)
    received = halo(polar)
    screened = call(screen_kernel, half, polar, *coulomb)
    if halos:
        screened = call(
            functools.partial(screen_halo_kernel, halos),
            half,
            place,
            screened,
            *received,
            *coulomb,
            scalars=True,
        )
    screened_hat = exchange(screened)
    sigma = exchange(call(functools.partial(convolve_kernel, scaling / points), half, lesser_hat, screened_hat))
    received = halo(sigma)
    out = call(output_kernel, shape(retarded_diag.shape), sigma, *retarded)
    if halos:
        out = call(
            functools.partial(output_halo_kernel, halos),
            shape(out.shape),
            place,
            out,
            *received,
            *retarded,
            scalars=True,
            out_specs=ANY,
            scratch_shapes=[
                pltpu.VMEM((halos, 2, orbitals, orbitals), f32),
                pltpu.SemaphoreType.DMA((2 * (cells + halos),)),
            ],
        )
    return out


def solution(mesh):
    over_both = P(None, "energy", "cell", None, None)
    over_cell = P("cell", None, None)
    return jax.shard_map(
        per_device,
        mesh=mesh,
        in_specs=(over_both, over_both, over_both, over_cell, over_cell),
        out_specs=over_both,
        check_vma=False,
    )
```

```python
import functools
import math

import jax
import jax.numpy as jnp
from jax import lax
from jax.experimental import pallas as pl
from jax.experimental.pallas import tpu as pltpu
from jax.sharding import PartitionSpec as P

VMEM = pl.BlockSpec(memory_space=pltpu.VMEM)
ANY = pl.BlockSpec(memory_space=pl.ANY)
f32 = jnp.float32
bf16 = jnp.bfloat16


def times_root(value, turn, points, sign):
    re, im = value
    turn = turn % points
    if turn == 0:
        return value
    if 4 * turn == points:
        return (-im, re) if sign > 0 else (im, -re)
    if 2 * turn == points:
        return (-re, -im)
    if 4 * turn == 3 * points:
        return (im, -re) if sign > 0 else (-im, re)
    angle = 2.0 * math.pi * turn / points
    c, s = math.cos(angle), sign * math.sin(angle)
    if 8 * turn % points == 0:
        unit = abs(c)
        a = re if c > 0 else -re
        b = im if c > 0 else -im
        if (s > 0) == (c > 0):
            return ((a - b) * unit, (a + b) * unit)
        return ((a + b) * unit, (b - a) * unit)
    return (re * c - im * s, re * s + im * c)


def fourier(values, sign):
    points = len(values)
    if points == 1:
        return values
    if points % 2:
        out = []
        for k in range(points):
            total = values[0]
            for n in range(1, points):
                term = times_root(values[n], k * n, points, sign)
                total = (total[0] + term[0], total[1] + term[1])
            out.append(total)
        return out
    even = fourier(values[0::2], sign)
    odd = fourier(values[1::2], sign)
    low, high = [], []
    for k in range(points // 2):
        a = even[k]
        b = times_root(odd[k], k, points, sign)
        low.append((a[0] + b[0], a[1] + b[1]))
        high.append((a[0] - b[0], a[1] - b[1]))
    return low + high


def tiles_of(cells, rows, lanes):
    step_rows = 8 if rows % 8 == 0 else rows
    step_lanes = 128 if lanes % 128 == 0 else lanes
    return [
        (c, pl.ds(r, step_rows), pl.ds(b, step_lanes))
        for c in range(cells)
        for r in range(0, rows, step_rows)
        for b in range(0, lanes, step_lanes)
    ]


def polarize_kernel(scaling, entries, lesser_hat, polar_hat):
    points, _, cells, rows, lanes = entries.shape
    at = places_of(points)
    for c, r, b in tiles_of(cells, rows, lanes):
        hats = []
        for pair in (0, 2):
            hats.append(fourier([(entries[i, pair, c, r, b], entries[i, pair + 1, c, r, b]) for i in at], -1))
            if pair == 0:
                for k in range(points):
                    lesser_hat[k, 0, c, r, b] = hats[0][k][0]
                    lesser_hat[k, 1, c, r, b] = hats[0][k][1]
        for k in range(points):
            greater_re, greater_im = hats[1][k]
            lesser_re = lesser_hat[k, 0, c, r, b]
            lesser_im = lesser_hat[k, 1, c, r, b]
            polar_hat[at[k], 0, c, r, b] = (lesser_re * greater_im - lesser_im * greater_re) * scaling
            polar_hat[at[k], 1, c, r, b] = (lesser_re * greater_re + lesser_im * greater_im) * scaling


def convolve_kernel(factor, lesser_hat, screened_hat, sigma):
    points, _, cells, rows, lanes = screened_hat.shape
    at = places_of(points)
    for c, r, b in tiles_of(cells, rows, lanes):
        spectral = []
        for k in range(points):
            lesser_re, lesser_im = lesser_hat[k, 0, c, r, b], lesser_hat[k, 1, c, r, b]
            w_re, w_im = screened_hat[at[k], 0, c, r, b], screened_hat[at[k], 1, c, r, b]
            spectral.append(
                ((lesser_re * w_re - lesser_im * w_im) * factor, (lesser_re * w_im + lesser_im * w_re) * factor)
            )
        for n, (re, im) in enumerate(fourier(spectral, 1)):
            sigma[at[n], 0, c, r, b] = -im
            sigma[at[n], 1, c, r, b] = re


def parts(matrix):
    high = matrix.astype(bf16)
    return (high, (matrix - high.astype(f32)).astype(bf16))


def join(pieces, axis):
    return tuple(jnp.concatenate(p, axis) for p in zip(*pieces, strict=True))


def negative(pair):
    return tuple(-p for p in pair)


def product(left, right, turned=False):
    dims = (((1,), (1 if turned else 0,)), ((), ()))
    dot = functools.partial(lax.dot_general, dimension_numbers=dims, preferred_element_type=f32)
    return dot(left[0], right[0]) + (dot(left[0], right[1]) + dot(left[1], right[0]))


def block_of(ref, plane, cell):
    slabs, _, _, rows, lanes = ref.shape
    return ref[:, plane, cell].reshape(slabs * rows, lanes)


def local_terms(cells):
    terms = [(c, c, c) for c in range(cells)]
    for c in range(cells - 1):
        terms.append((c, c + 1, cells + 2 * c))
        terms.append((c + 1, c, cells + 2 * c + 1))
    return sorted(terms)


def matrices_kernel(cells, halos, place, *refs):
    c_diag, c_upper, r_diag, r_upper, c_edge, r_edge = refs[:6]
    c_high, c_low, r_high, r_low = refs[6:]

    def store(ref, i, matrix):
        for out, part in zip(ref, parts(matrix), strict=True):
            out[i] = part

    def fill(refs, read_diag, read_upper, edge):
        for c in range(cells):
            store(refs, c, read_diag(c))
        for c in range(cells - 1):
            store(refs, cells + 2 * c, read_upper(c))
            store(refs, cells + 2 * c + 1, read_upper(c).T)
        first = 3 * cells - 2
        if halos == 1:
            store(refs, first, jnp.where(place[1] == 0, read_upper(cells - 1), edge.T))
        if halos == 2:
            store(refs, first, edge.T)
            store(refs, first + 1, read_upper(cells - 1))

    fill((c_high, c_low), lambda c: (c_diag[c] + c_diag[c].T) * 0.5, lambda c: c_upper[c], c_edge[...])
    for p in range(2):
        fill(
            (r_high.at[p], r_low.at[p]),
            lambda c, p=p: r_diag[p, 0, c],
            lambda c, p=p: r_upper[p, 0, c],
            r_edge[p],
        )


def real_terms(high, low, terms, read, planes):
    lefts, inners = [], []
    for source, i in terms:
        left = (high[i], low[i])
        stacked = parts(jnp.concatenate([read(p, source) for p in range(planes)], 0))
        lefts.append(left)
        inners.append(parts(product(stacked, left, True)))
    left = join(lefts, 1)
    lanes = high.shape[-1]
    return [
        product(left, join([tuple(q[p * lanes : (p + 1) * lanes] for q in i) for i in inners], 0))
        for p in range(planes)
    ]


def complex_terms(high, low, terms, read, on_real=None):
    out_re, out_im = None, None
    for source, i in terms:
        re, im = ((high[p, i], low[p, i]) for p in range(2))
        whole_re, whole_im = (sum(q.astype(f32) for q in pair) for pair in (re, im))
        both, apart = parts(whole_re + whole_im), parts(whole_re - whole_im)
        x_re, x_im = read(0, source), read(1, source)
        a, b = product(re, parts(x_re)), product(im, parts(x_im))
        c = product(both, parts(x_re + x_im))
        t_re, t_im = a - b, c - a - b
        a, b = product(parts(t_re), re, True), product(parts(t_im), im, True)
        out_re = a + b if out_re is None else out_re + (a + b)
        if on_real is not None and (source, i) == terms[-1]:
            on_real(out_re)
        c = product(parts(t_re + t_im), apart, True)
        out_im = c - a + b if out_im is None else out_im + (c - a + b)
    return out_re, out_im


def real_term(left, blocks):
    lanes = left[0].shape[-1]
    first = parts(product(left, parts(jnp.concatenate(blocks, 1))))
    count = len(blocks)
    stacked = tuple(jnp.concatenate([q[:, p * lanes : (p + 1) * lanes] for p in range(count)], 0) for q in first)
    total = product(stacked, left, True)
    return [total[p * lanes : (p + 1) * lanes] for p in range(count)]


def screen_kernel(here, high, low, out):
    slabs, planes, cells, rows, lanes = here.shape
    for c in range(cells):
        terms = [(source, i) for target, source, i in local_terms(cells) if target == c]
        sums = real_terms(high, low, terms, lambda p, source: block_of(here, p, source), planes)
        for p, total in enumerate(sums):
            out[:, p, c] = total.reshape(slabs, rows, lanes)


def screen_halo_kernel(halos, place, before, *refs):
    received, high, low, out = refs[:halos], refs[halos], refs[halos + 1], refs[halos + 2]
    slabs, planes, cells, rows, lanes = out.shape
    for c in range(cells):

        @pl.when(untouched(halos, place, c))
        def _(c=c):
            out[:, :, c] = before[:, :, c]

    for h in range(halos):
        i = 3 * cells - 2 + h
        sums = real_term((high[i], low[i]), [block_of(received[h], p, 0) for p in range(planes)])
        c = place[2 + h]
        for p, total in enumerate(sums):
            out[:, p, c] = before[:, p, c] + total.reshape(slabs, rows, lanes)


def untouched(halos, place, c):
    return functools.reduce(jnp.logical_and, [place[2 + h] != c for h in range(halos)])


def output_kernel(here, high, low, out):
    cells = here.shape[2]
    for c in range(cells):
        terms = [(source, i) for target, source, i in local_terms(cells) if target == c]
        out[0, 0, c], out[1, 0, c] = complex_terms(high, low, terms, lambda p, source: block_of(here, p, source))


def output_halo_kernel(halos, place, before, *refs):
    received, high, low, out = refs[:halos], refs[halos], refs[halos + 1], refs[halos + 2]
    total, sems = refs[halos + 3 :]
    cells = out.shape[2]

    def copy_of(ref, p, c, i):
        return pltpu.make_async_copy(ref, out.at[p, 0, c], sems.at[i])

    def kept(c):
        return [copy_of(before.at[p, 0, c], p, c, 2 * c + p) for p in range(2)]

    def added(h):
        return [copy_of(total.at[h, p], p, place[2 + h], 2 * (cells + h) + p) for p in range(2)]

    for c in range(cells):

        @pl.when(untouched(halos, place, c))
        def _(c=c):
            for copy in kept(c):
                copy.start()

    for h in range(halos):
        terms = [(0, 3 * cells - 2 + h)]
        c = place[2 + h]

        def send(p, value, h=h, c=c):
            total[h, p] = before[p, 0, c] + value
            added(h)[p].start()

        sums = complex_terms(
            high,
            low,
            terms,
            lambda p, source, h=h: block_of(received[h], p, source),
            functools.partial(send, 0),
        )
        send(1, sums[1])
    for c in range(cells):

        @pl.when(untouched(halos, place, c))
        def _(c=c):
            for copy in kept(c):
                copy.wait()

    for h in range(halos):
        for copy in added(h):
            copy.wait()


def slabs_kernel(green, slabs, stage, sems_in, sems_out):
    devices, planes, cells, rows, lanes = slabs.shape
    blocks = [(p, c) for p in range(planes) for c in range(cells)]
    into = [
        pltpu.make_async_copy(green.at[p, 0, c], stage.at[i], sems_in.at[i])
        for i, (p, c) in enumerate(blocks)
    ]
    out = [pltpu.make_async_copy(stage.at[i], slabs.at[:, p, c], sems_out.at[i]) for i, (p, c) in enumerate(blocks)]
    for copy in into:
        copy.start()
    for first, second in zip(into, out, strict=True):
        first.wait()
        second.start()
    for copy in out:
        copy.wait()


def call(kernel, outs, *args, scalars=False, out_specs=None, **more):
    first = [pl.BlockSpec(memory_space=pltpu.SMEM)] if scalars else []
    return pl.pallas_call(
        kernel,
        out_shape=outs,
        in_specs=first + [VMEM] * (len(args) - len(first)),
        out_specs=out_specs or jax.tree.map(lambda _: VMEM, outs),
        compiler_params=pltpu.CompilerParams(vmem_limit_bytes=32 * 1024 * 1024),
        **more,
    )(*args)


def shape(dims):
    return jax.ShapeDtypeStruct(tuple(dims), f32)


def order_of(devices):
    return [(e + devices // 2 + 1) % devices for e in range(devices)]


def places_of(points):
    order = order_of(points)
    return [order.index(e) for e in range(points)]


def exchange(values):
    order = order_of(lax.axis_size("energy"))
    return lax.all_to_all(
        values, "energy", split_axis=0, concat_axis=0, axis_index_groups=[order], tiled=True
    )


def shifted(block, axis, step):
    count = lax.axis_size(axis)
    route = [(i, i + step) for i in range(count) if 0 <= i + step < count]
    return lax.ppermute(block, axis, route)


def swapped(block):
    return lax.ppermute(block, "cell", [(0, 1), (1, 0)])


def halo(values):
    count = lax.axis_size("cell")
    if count == 1:
        return []
    head, tail = values[:, :, :1], values[:, :, -1:]
    if count == 2:
        return [swapped(jnp.where(lax.axis_index("cell") == 0, tail, head))]
    return [shifted(tail, "cell", 1), shifted(head, "cell", -1)]


def place_of(cells):
    count, index = lax.axis_size("cell"), lax.axis_index("cell")
    if count == 1:
        targets = []
    elif count == 2:
        targets = [jnp.where(index == 0, cells - 1, 0)]
    else:
        targets = [0, cells - 1]
    return len(targets), jnp.stack([jnp.asarray(v, jnp.int32) for v in [len(targets), index, *targets]])


def per_device(green_pair, retarded_diag, retarded_upper, coulomb_diag, coulomb_upper):
    devices = lax.axis_size("energy")
    _, held, cells, orbitals, _ = green_pair.shape
    points = devices * held
    scaling = 1.0 / math.sqrt(points)
    rows = orbitals // devices
    halos, place = place_of(cells)
    count = 3 * cells - 2 + halos
    part = jax.ShapeDtypeStruct((count, orbitals, orbitals), bf16)
    pair = jax.ShapeDtypeStruct((2, count, orbitals, orbitals), bf16)
    matrices = call(
        functools.partial(matrices_kernel, cells, halos),
        (part, part, pair, pair),
        place,
        coulomb_diag,
        coulomb_upper,
        retarded_diag,
        retarded_upper,
        shifted(coulomb_upper[-1], "cell", 1),
        shifted(retarded_upper[:, 0, -1], "cell", 1),
        scalars=True,
        cost_estimate=pl.CostEstimate(flops=10**9, bytes_accessed=16 * count * orbitals**2 * 4, transcendentals=0),
    )
    slabs = pl.pallas_call(
        slabs_kernel,
        out_shape=shape((devices, 4, cells, rows, orbitals)),
        in_specs=[ANY],
        out_specs=ANY,
        scratch_shapes=[
            pltpu.VMEM((4 * cells, devices, rows, orbitals), f32),
            pltpu.SemaphoreType.DMA((4 * cells,)),
            pltpu.SemaphoreType.DMA((4 * cells,)),
        ],
    )(green_pair.reshape(4, held, cells, devices, rows, orbitals))
    entries, matrices = lax.optimization_barrier((exchange(slabs), matrices))
    coulomb, retarded = matrices[:2], matrices[2:]
    half = shape((points, 2, cells, rows, orbitals))
    lesser_hat, polar_hat = call(functools.partial(polarize_kernel, scaling), (half, half), entries)
    polar = exchange(polar_hat)
    received = halo(polar)
    screened = call(screen_kernel, half, polar, *coulomb)
    if halos:
        screened = call(
            functools.partial(screen_halo_kernel, halos),
            half,
            place,
            screened,
            *received,
            *coulomb,
            scalars=True,
        )
    screened_hat = exchange(screened)
    sigma = exchange(call(functools.partial(convolve_kernel, scaling / points), half, lesser_hat, screened_hat))
    received = halo(sigma)
    out = call(output_kernel, shape(retarded_diag.shape), sigma, *retarded)
    if halos:
        out = call(
            functools.partial(output_halo_kernel, halos),
            shape(out.shape),
            place,
            out,
            *received,
            *retarded,
            scalars=True,
            out_specs=ANY,
            scratch_shapes=[
                pltpu.VMEM((halos, 2, orbitals, orbitals), f32),
                pltpu.SemaphoreType.DMA((2 * (cells + halos),)),
            ],
        )
    return out


def solution(mesh):
    over_both = P(None, "energy", "cell", None, None)
    over_cell = P("cell", None, None)
    return jax.shard_map(
        per_device,
        mesh=mesh,
        in_specs=(over_both, over_both, over_both, over_cell, over_cell),
        out_specs=over_both,
        check_vma=False,
    )
```

```python
import functools
import math

import jax
import jax.numpy as jnp
from jax import lax
from jax.experimental import pallas as pl
from jax.experimental.pallas import tpu as pltpu
from jax.sharding import PartitionSpec as P

VMEM = pl.BlockSpec(memory_space=pltpu.VMEM)
ANY = pl.BlockSpec(memory_space=pl.ANY)
f32 = jnp.float32
bf16 = jnp.bfloat16


def times_root(value, turn, points, sign):
    re, im = value
    turn = turn % points
    if turn == 0:
        return value
    if 4 * turn == points:
        return (-im, re) if sign > 0 else (im, -re)
    if 2 * turn == points:
        return (-re, -im)
    if 4 * turn == 3 * points:
        return (im, -re) if sign > 0 else (-im, re)
    angle = 2.0 * math.pi * turn / points
    c, s = math.cos(angle), sign * math.sin(angle)
    if 8 * turn % points == 0:
        unit = abs(c)
        a = re if c > 0 else -re
        b = im if c > 0 else -im
        if (s > 0) == (c > 0):
            return ((a - b) * unit, (a + b) * unit)
        return ((a + b) * unit, (b - a) * unit)
    return (re * c - im * s, re * s + im * c)


def fourier(values, sign):
    points = len(values)
    if points == 1:
        return values
    if points % 2:
        out = []
        for k in range(points):
            total = values[0]
            for n in range(1, points):
                term = times_root(values[n], k * n, points, sign)
                total = (total[0] + term[0], total[1] + term[1])
            out.append(total)
        return out
    even = fourier(values[0::2], sign)
    odd = fourier(values[1::2], sign)
    low, high = [], []
    for k in range(points // 2):
        a = even[k]
        b = times_root(odd[k], k, points, sign)
        low.append((a[0] + b[0], a[1] + b[1]))
        high.append((a[0] - b[0], a[1] - b[1]))
    return low + high


def tiles_of(cells, rows, lanes):
    step_rows = 8 if rows % 8 == 0 else rows
    step_lanes = 128 if lanes % 128 == 0 else lanes
    return [
        (c, pl.ds(r, step_rows), pl.ds(b, step_lanes))
        for c in range(cells)
        for r in range(0, rows, step_rows)
        for b in range(0, lanes, step_lanes)
    ]


def polarize_kernel(scaling, entries, lesser_hat, polar_hat):
    points, _, cells, rows, lanes = entries.shape
    at = places_of(points)
    for c, r, b in tiles_of(cells, rows, lanes):
        hats = []
        for pair in (0, 2):
            hats.append(fourier([(entries[i, pair, c, r, b], entries[i, pair + 1, c, r, b]) for i in at], -1))
            if pair == 0:
                for k in range(points):
                    lesser_hat[k, 0, c, r, b] = hats[0][k][0]
                    lesser_hat[k, 1, c, r, b] = hats[0][k][1]
        for k in range(points):
            greater_re, greater_im = hats[1][k]
            lesser_re = lesser_hat[k, 0, c, r, b]
            lesser_im = lesser_hat[k, 1, c, r, b]
            polar_hat[at[k], 0, c, r, b] = (lesser_re * greater_im - lesser_im * greater_re) * scaling
            polar_hat[at[k], 1, c, r, b] = (lesser_re * greater_re + lesser_im * greater_im) * scaling


def convolve_kernel(factor, lesser_hat, screened_hat, sigma):
    points, _, cells, rows, lanes = screened_hat.shape
    at = places_of(points)
    for c, r, b in tiles_of(cells, rows, lanes):
        spectral = []
        for k in range(points):
            lesser_re, lesser_im = lesser_hat[k, 0, c, r, b], lesser_hat[k, 1, c, r, b]
            w_re, w_im = screened_hat[at[k], 0, c, r, b], screened_hat[at[k], 1, c, r, b]
            spectral.append(
                ((lesser_re * w_re - lesser_im * w_im) * factor, (lesser_re * w_im + lesser_im * w_re) * factor)
            )
        for n, (re, im) in enumerate(fourier(spectral, 1)):
            sigma[at[n], 0, c, r, b] = -im
            sigma[at[n], 1, c, r, b] = re


def parts(matrix):
    high = matrix.astype(bf16)
    return (high, (matrix - high.astype(f32)).astype(bf16))


def join(pieces, axis):
    return tuple(jnp.concatenate(p, axis) for p in zip(*pieces, strict=True))


def negative(pair):
    return tuple(-p for p in pair)


def product(left, right, turned=False):
    dims = (((1,), (1 if turned else 0,)), ((), ()))
    dot = functools.partial(lax.dot_general, dimension_numbers=dims, preferred_element_type=f32)
    return dot(left[0], right[0]) + (dot(left[0], right[1]) + dot(left[1], right[0]))


def block_of(ref, plane, cell):
    slabs, _, _, rows, lanes = ref.shape
    return ref[:, plane, cell].reshape(slabs * rows, lanes)


def local_terms(cells):
    terms = [(c, c, c) for c in range(cells)]
    for c in range(cells - 1):
        terms.append((c, c + 1, cells + 2 * c))
        terms.append((c + 1, c, cells + 2 * c + 1))
    return sorted(terms)


def matrices_kernel(cells, halos, place, *refs):
    c_diag, c_upper, r_diag, r_upper, c_edge, r_edge = refs[:6]
    c_high, c_low, r_high, r_low = refs[6:]

    def store(ref, i, matrix):
        for out, part in zip(ref, parts(matrix), strict=True):
            out[i] = part

    def fill(refs, read_diag, read_upper, edge):
        for c in range(cells):
            store(refs, c, read_diag(c))
        for c in range(cells - 1):
            store(refs, cells + 2 * c, read_upper(c))
            store(refs, cells + 2 * c + 1, read_upper(c).T)
        first = 3 * cells - 2
        if halos == 1:
            store(refs, first, jnp.where(place[1] == 0, read_upper(cells - 1), edge.T))
        if halos == 2:
            store(refs, first, edge.T)
            store(refs, first + 1, read_upper(cells - 1))

    fill((c_high, c_low), lambda c: (c_diag[c] + c_diag[c].T) * 0.5, lambda c: c_upper[c], c_edge[...])
    for p in range(2):
        fill(
            (r_high.at[p], r_low.at[p]),
            lambda c, p=p: r_diag[p, 0, c],
            lambda c, p=p: r_upper[p, 0, c],
            r_edge[p],
        )


def real_terms(high, low, terms, read, planes):
    lefts, inners = [], []
    for source, i in terms:
        left = (high[i], low[i])
        stacked = parts(jnp.concatenate([read(p, source) for p in range(planes)], 0))
        lefts.append(left)
        inners.append(parts(product(stacked, left, True)))
    left = join(lefts, 1)
    lanes = high.shape[-1]
    return [
        product(left, join([tuple(q[p * lanes : (p + 1) * lanes] for q in i) for i in inners], 0))
        for p in range(planes)
    ]


def complex_terms(high, low, terms, read, on_real=None):
    out_re, out_im = None, None
    for source, i in terms:
        re, im = ((high[p, i], low[p, i]) for p in range(2))
        whole_re, whole_im = (sum(q.astype(f32) for q in pair) for pair in (re, im))
        both, apart = parts(whole_re + whole_im), parts(whole_re - whole_im)
        x_re, x_im = read(0, source), read(1, source)
        a, b = product(re, parts(x_re)), product(im, parts(x_im))
        c = product(both, parts(x_re + x_im))
        t_re, t_im = a - b, c - a - b
        a, b = product(parts(t_re), re, True), product(parts(t_im), im, True)
        out_re = a + b if out_re is None else out_re + (a + b)
        if on_real is not None and (source, i) == terms[-1]:
            on_real(out_re)
        c = product(parts(t_re + t_im), apart, True)
        out_im = c - a + b if out_im is None else out_im + (c - a + b)
    return out_re, out_im


def real_term(left, blocks):
    lanes = left[0].shape[-1]
    first = parts(product(left, parts(jnp.concatenate(blocks, 1))))
    count = len(blocks)
    stacked = tuple(jnp.concatenate([q[:, p * lanes : (p + 1) * lanes] for p in range(count)], 0) for q in first)
    total = product(stacked, left, True)
    return [total[p * lanes : (p + 1) * lanes] for p in range(count)]


def screen_kernel(here, high, low, out):
    slabs, planes, cells, rows, lanes = here.shape
    for c in range(cells):
        terms = [(source, i) for target, source, i in local_terms(cells) if target == c]
        sums = real_terms(high, low, terms, lambda p, source: block_of(here, p, source), planes)
        for p, total in enumerate(sums):
            out[:, p, c] = total.reshape(slabs, rows, lanes)


def screen_halo_kernel(halos, place, before, *refs):
    received, high, low, out = refs[:halos], refs[halos], refs[halos + 1], refs[halos + 2]
    slabs, planes, cells, rows, lanes = out.shape
    for c in range(cells):

        @pl.when(untouched(halos, place, c))
        def _(c=c):
            out[:, :, c] = before[:, :, c]

    for h in range(halos):
        i = 3 * cells - 2 + h
        sums = real_term((high[i], low[i]), [block_of(received[h], p, 0) for p in range(planes)])
        c = place[2 + h]
        for p, total in enumerate(sums):
            out[:, p, c] = before[:, p, c] + total.reshape(slabs, rows, lanes)


def untouched(halos, place, c):
    return functools.reduce(jnp.logical_and, [place[2 + h] != c for h in range(halos)])


def output_kernel(here, high, low, out):
    cells = here.shape[2]
    for c in range(cells):
        terms = [(source, i) for target, source, i in local_terms(cells) if target == c]
        out[0, 0, c], out[1, 0, c] = complex_terms(high, low, terms, lambda p, source: block_of(here, p, source))


def output_halo_kernel(halos, place, before, *refs):
    received, high, low, out = refs[:halos], refs[halos], refs[halos + 1], refs[halos + 2]
    total, sems = refs[halos + 3 :]
    cells = out.shape[2]

    def copy_of(ref, p, c, i):
        return pltpu.make_async_copy(ref, out.at[p, 0, c], sems.at[i])

    def kept(c):
        return pltpu.make_async_copy(before.at[:, :, c], out.at[:, :, c], sems.at[c])

    def added(h, p):
        return copy_of(total.at[h, p], p, place[2 + h], cells + 2 * h + p)

    for c in range(cells):

        @pl.when(untouched(halos, place, c))
        def _(c=c):
            kept(c).start()

    for h in range(halos):
        terms = [(0, 3 * cells - 2 + h)]
        c = place[2 + h]

        def send(p, value, h=h, c=c):
            total[h, p] = before[p, 0, c] + value
            added(h, p).start()

        sums = complex_terms(
            high,
            low,
            terms,
            lambda p, source, h=h: block_of(received[h], p, source),
            functools.partial(send, 0),
        )
        send(1, sums[1])
    for c in range(cells):

        @pl.when(untouched(halos, place, c))
        def _(c=c):
            kept(c).wait()

    for h in range(halos):
        for p in range(2):
            added(h, p).wait()


def slabs_kernel(green, slabs, stage, sems_in, sems_out):
    devices, planes, cells, rows, lanes = slabs.shape
    blocks = [(p, c) for p in range(planes) for c in range(cells)]
    into = [
        pltpu.make_async_copy(green.at[p, 0, c], stage.at[i], sems_in.at[i])
        for i, (p, c) in enumerate(blocks)
    ]
    out = [pltpu.make_async_copy(stage.at[i], slabs.at[:, p, c], sems_out.at[i]) for i, (p, c) in enumerate(blocks)]
    for copy in into:
        copy.start()
    for first, second in zip(into, out, strict=True):
        first.wait()
        second.start()
    for copy in out:
        copy.wait()


def call(kernel, outs, *args, scalars=False, out_specs=None, **more):
    first = [pl.BlockSpec(memory_space=pltpu.SMEM)] if scalars else []
    return pl.pallas_call(
        kernel,
        out_shape=outs,
        in_specs=first + [VMEM] * (len(args) - len(first)),
        out_specs=out_specs or jax.tree.map(lambda _: VMEM, outs),
        compiler_params=pltpu.CompilerParams(vmem_limit_bytes=16 * 1024 * 1024),
        **more,
    )(*args)


def shape(dims):
    return jax.ShapeDtypeStruct(tuple(dims), f32)


def order_of(devices):
    return [(e + devices // 2 + 1) % devices for e in range(devices)]


def places_of(points):
    order = order_of(points)
    return [order.index(e) for e in range(points)]


def exchange(values):
    order = order_of(lax.axis_size("energy"))
    return lax.all_to_all(
        values, "energy", split_axis=0, concat_axis=0, axis_index_groups=[order], tiled=True
    )


def shifted(block, axis, step):
    count = lax.axis_size(axis)
    route = [(i, i + step) for i in range(count) if 0 <= i + step < count]
    return lax.ppermute(block, axis, route)


def swapped(block):
    return lax.ppermute(block, "cell", [(0, 1), (1, 0)])


def halo(values):
    count = lax.axis_size("cell")
    if count == 1:
        return []
    head, tail = values[:, :, :1], values[:, :, -1:]
    if count == 2:
        return [swapped(jnp.where(lax.axis_index("cell") == 0, tail, head))]
    return [shifted(tail, "cell", 1), shifted(head, "cell", -1)]


def place_of(cells):
    count, index = lax.axis_size("cell"), lax.axis_index("cell")
    if count == 1:
        targets = []
    elif count == 2:
        targets = [jnp.where(index == 0, cells - 1, 0)]
    else:
        targets = [0, cells - 1]
    return len(targets), jnp.stack([jnp.asarray(v, jnp.int32) for v in [len(targets), index, *targets]])


def per_device(green_pair, retarded_diag, retarded_upper, coulomb_diag, coulomb_upper):
    devices = lax.axis_size("energy")
    _, held, cells, orbitals, _ = green_pair.shape
    points = devices * held
    scaling = 1.0 / math.sqrt(points)
    rows = orbitals // devices
    halos, place = place_of(cells)
    count = 3 * cells - 2 + halos
    part = jax.ShapeDtypeStruct((count, orbitals, orbitals), bf16)
    pair = jax.ShapeDtypeStruct((2, count, orbitals, orbitals), bf16)
    matrices = call(
        functools.partial(matrices_kernel, cells, halos),
        (part, part, pair, pair),
        place,
        coulomb_diag,
        coulomb_upper,
        retarded_diag,
        retarded_upper,
        shifted(coulomb_upper[-1], "cell", 1),
        shifted(retarded_upper[:, 0, -1], "cell", 1),
        scalars=True,
        cost_estimate=pl.CostEstimate(flops=10**9, bytes_accessed=16 * count * orbitals**2 * 4, transcendentals=0),
    )
    slabs = pl.pallas_call(
        slabs_kernel,
        out_shape=shape((devices, 4, cells, rows, orbitals)),
        in_specs=[ANY],
        out_specs=ANY,
        scratch_shapes=[
            pltpu.VMEM((4 * cells, devices, rows, orbitals), f32),
            pltpu.SemaphoreType.DMA((4 * cells,)),
            pltpu.SemaphoreType.DMA((4 * cells,)),
        ],
    )(green_pair.reshape(4, held, cells, devices, rows, orbitals))
    entries, matrices = lax.optimization_barrier((exchange(slabs), matrices))
    coulomb, retarded = matrices[:2], matrices[2:]
    half = shape((points, 2, cells, rows, orbitals))
    lesser_hat, polar_hat = call(functools.partial(polarize_kernel, scaling), (half, half), entries)
    polar = exchange(polar_hat)
    received = halo(polar)
    screened = call(screen_kernel, half, polar, *coulomb)
    if halos:
        screened = call(
            functools.partial(screen_halo_kernel, halos),
            half,
            place,
            screened,
            *received,
            *coulomb,
            scalars=True,
        )
    screened_hat = exchange(screened)
    sigma = exchange(call(functools.partial(convolve_kernel, scaling / points), half, lesser_hat, screened_hat))
    received = halo(sigma)
    out = call(output_kernel, shape(retarded_diag.shape), sigma, *retarded)
    if halos:
        out = call(
            functools.partial(output_halo_kernel, halos),
            shape(out.shape),
            place,
            out,
            *received,
            *retarded,
            scalars=True,
            out_specs=ANY,
            scratch_shapes=[
                pltpu.VMEM((halos, 2, orbitals, orbitals), f32),
                pltpu.SemaphoreType.DMA((cells + 2 * halos,)),
            ],
        )
    return out


def solution(mesh):
    over_both = P(None, "energy", "cell", None, None)
    over_cell = P("cell", None, None)
    return jax.shard_map(
        per_device,
        mesh=mesh,
        in_specs=(over_both, over_both, over_both, over_cell, over_cell),
        out_specs=over_both,
        check_vma=False,
    )
```
